128 devices in a mesh: dom: 128 (over x, y, z, core).
Axes of the slice: x: 4, y: 4, z: 4, core: 2. Of those that a mesh axis runs over, the one named last changes fastest.
Arguments:
- features: bfloat16 [262144, 256], P('dom'), may hold values from -24 to 24
- self_weight: bfloat16 [256, 256], replicated, may hold values from -0.375 to 0.375
- neighbour_weight: bfloat16 [256, 256], replicated, may hold values from -0.375 to 0.375
- send_lists: int32 [128, 128, 8], P('dom'), may hold values from 0 to 2047
- hub_nodes: int32 [128, 8], P('dom'), may hold values from 0 to 2047
- neighbours: int32 [262144, 16], P('dom'), may hold values from 0 to 4095
- counts: int32 [262144], P('dom'), may hold values from 1 to 16
- cotangent: bfloat16 [262144, 256], P('dom'), may hold values from -6 to 6
Outputs:
- activations: bfloat16 [262144, 256], P('dom')
- grad_features: float32 [262144, 256], P('dom')
- grad_weights: float32 [512, 256], P('dom')
The draws below stay inside these ranges and needn't reach their ends.
All inputs are finite; a program needn't handle non-finite values.
Results may differ from the reference program's by a relative error of at most 0.0032.
Values may be sent and summed in bfloat16 or wider, within the bound.
No kernel may reach another device: no remote copies, remote signals or barrier semaphores. Data moves between devices by JAX's collectives and lax.ppermute only.
A program may use at most 64 MiB of HBM per device.

```python
import jax
import jax.numpy as jnp
from jax import lax

F = 256
H = 256
FAN = 16
NODE_DEV = 2048
BND = 8
HUB_DEV = 8
NODES = 262144
TABLE = 4096
N_DOM = 128


def place_ends(drawn, stream_key, least, largest):
    index_at = [jax.random.randint(jax.random.fold_in(stream_key, axis), (), 0, length) for axis, length in enumerate(drawn.shape)]
    longest = drawn.shape.index(max(drawn.shape))
    beside = index_at[:longest] + [(index_at[longest] + 1) % drawn.shape[longest]] + index_at[longest + 1:]
    return drawn.at[tuple(index_at)].set(least).at[tuple(beside)].set(largest)


def raised(result, rng, source, target, parts, factor):
    owner, partner = [(jnp.arange(result.shape[dim]) // (result.shape[dim] // parts)).reshape([-1 if axis == dim else 1 for axis in range(result.ndim)]) for dim in (source, target)]
    chosen = jax.random.permutation(rng, parts)[partner]
    strong = (owner == chosen) | (owner == (partner + parts // 2) % parts)
    return jnp.where(strong, factor * result, result)


def block_levels(own_key, shape, shards, least, high):
    level, own = 1.0, jax.random.fold_in(own_key, 6)
    for position, blocks in shards:
        draws = jnp.exp(jax.random.uniform(jax.random.fold_in(own, position), (blocks,), jnp.float32, least / len(shards), high / len(shards)))
        level = level * jnp.repeat(draws, shape[position] // blocks).reshape([-1 if axis == position else 1 for axis in range(len(shape))])
    return level


def bell_draw(stream_key, shape, spread, limit, pieces=(), kind=jnp.bfloat16):
    array = jax.random.normal(stream_key, shape, jnp.float32) * spread
    if len(pieces) > 0:
        array = block_levels(stream_key, shape, pieces, -0.22, 0.18) * array
    return jnp.clip(array, min=-limit, max=limit).astype(kind)


def noise_with(key, extent, width, limit, shards, heavy, held_as=jnp.bfloat16):
    result = width * jax.random.normal(key, extent, jnp.float32)
    if shards:
        result = result * block_levels(key, extent, shards, -0.22, 0.18)
    return jnp.clip(raised(result, jax.random.fold_in(key, 3), *heavy), -limit, limit).astype(held_as)


def setup_inputs(seed: int = 0) -> dict:
    splits = jax.random.split(jax.random.key(seed), 9)
    features = noise_with(splits[0], (NODES, F), 1.0, 24.0, ((0, 128),), (0, 1, 128, 5.5))
    self_weight = bell_draw(splits[1], (F, H), F ** -0.5, 0.375)
    neighbour_weight = bell_draw(splits[2], (F, H), F ** -0.5, 0.375)
    send_lists = place_ends(jax.random.randint(splits[3], (N_DOM, N_DOM, BND), 0, NODE_DEV), jax.random.fold_in(splits[3], 1), 0, NODE_DEV - 1).astype(jnp.int32)
    hub_nodes = place_ends(jax.random.randint(splits[4], (N_DOM, HUB_DEV), 0, NODE_DEV), jax.random.fold_in(splits[4], 1), 0, NODE_DEV - 1).astype(jnp.int32)
    neighbours = place_ends(jax.random.randint(splits[5], (NODES, FAN), 0, TABLE), jax.random.fold_in(splits[5], 1), 0, TABLE - 1).astype(jnp.int32)
    counts = place_ends(jax.random.randint(splits[6], (NODES,), 1, FAN + 1), jax.random.fold_in(splits[6], 1), 1, FAN).astype(jnp.int32)
    cotangent = bell_draw(splits[7], (NODES, H), 1.0, 6.0, ((0, 128),))
    return dict(features=features, self_weight=self_weight, neighbour_weight=neighbour_weight, send_lists=send_lists, hub_nodes=hub_nodes, neighbours=neighbours, counts=counts, cotangent=cotangent)


def resolve(send_lists, hub_nodes, neighbours):
    partition = (jnp.arange(NODES, dtype=jnp.int32) // NODE_DEV)[:, None]
    table_slot = neighbours
    bound_slot = table_slot - NODE_DEV
    bound_peer = jnp.clip(bound_slot // BND, 0, N_DOM - 1)
    bound_pos = bound_slot % BND
    flat_lists = send_lists.reshape(-1)
    bound_index = (bound_peer * (N_DOM * BND) + partition * BND + bound_pos).astype(jnp.int32)
    bound_source = bound_peer * NODE_DEV + jnp.take(flat_lists, bound_index)
    hub_slot = table_slot - NODE_DEV - N_DOM * BND
    hub_owner = jnp.clip(hub_slot // HUB_DEV, 0, N_DOM - 1)
    hub_index = (hub_owner * HUB_DEV + hub_slot % HUB_DEV).astype(jnp.int32)
    hub_source = hub_owner * NODE_DEV + jnp.take(hub_nodes.reshape(-1), hub_index)
    local_source = partition * NODE_DEV + table_slot
    source = jnp.where(table_slot < NODE_DEV, local_source,
                       jnp.where(table_slot < NODE_DEV + N_DOM * BND, bound_source, hub_source))
    return source.astype(jnp.int32)


def reference(features, self_weight, neighbour_weight, send_lists, hub_nodes, neighbours, counts, cotangent):
    source = resolve(send_lists, hub_nodes, neighbours)
    usable = jnp.arange(FAN, dtype=jnp.int32)[None, :] < counts[:, None]
    degree = counts.astype(jnp.float32)[:, None]
    blocked_source = source.reshape(N_DOM, NODE_DEV, FAN)
    blocked_usable = usable.reshape(N_DOM, NODE_DEV, FAN)
    blocked_degree = degree.reshape(N_DOM, NODE_DEV, 1)

    def mean_block(block_args):
        block_source, block_usable, block_degree = block_args
        gathered = jnp.take(features, block_source, axis=0).astype(jnp.float32)
        summed = jnp.sum(jnp.where(block_usable[:, :, None], gathered, 0.0), axis=1)
        return (summed / block_degree).astype(jnp.bfloat16)

    mean = lax.map(mean_block, (blocked_source, blocked_usable, blocked_degree)).reshape(NODES, F)
    pre = jnp.dot(features, self_weight, preferred_element_type=jnp.float32) + jnp.dot(mean, neighbour_weight, preferred_element_type=jnp.float32)
    sigmoid_pre = jax.nn.sigmoid(pre)
    activations = (pre * sigmoid_pre).astype(jnp.bfloat16)
    grad_pre = (cotangent.astype(jnp.float32) * sigmoid_pre * (1.0 + pre * (1.0 - sigmoid_pre))).astype(jnp.bfloat16)
    grad_mean = jnp.dot(grad_pre, neighbour_weight.T, preferred_element_type=jnp.float32)
    grad_self = jnp.dot(grad_pre, self_weight.T, preferred_element_type=jnp.float32)
    edge_weight = (grad_mean / degree).reshape(N_DOM, NODE_DEV, F)

    def add_block(grad_total, block_args):
        block_source, block_usable, block_weight = block_args
        contrib = jnp.where(block_usable[:, :, None], block_weight[:, None, :], 0.0).reshape(-1, F)
        return grad_total.at[block_source.reshape(-1)].add(contrib), None

    grad_features, unused = lax.scan(add_block, grad_self, (blocked_source, blocked_usable, edge_weight))
    dims = (((0,), (0,)), ((), ()))
    upper = lax.dot_general(features, grad_pre, dims, preferred_element_type=jnp.float32)
    lower = lax.dot_general(mean, grad_pre, dims, preferred_element_type=jnp.float32)
    grad_weights = jnp.concatenate([upper, lower], axis=0)
    return activations, grad_features, grad_weights
```

```python
import jax
import jax.numpy as jnp
from jax import lax
from jax.experimental import pallas as pl
from jax.experimental.pallas import tpu as pltpu
from jax.sharding import PartitionSpec as P

BF16 = jnp.bfloat16
F32 = jnp.float32
I32 = jnp.int32
NODES = 2048
WIDTH = 256
PEERS = 128
SLOTS = 16
FAN = 16
GROUPS = NODES // 16
LOCAL = 8
REMOTE = 8
VMEM = pl.BlockSpec(memory_space=pltpu.VMEM)
NN = (((1,), (0,)), ((), ()))
NT = (((1,), (1,)), ((), ()))
TN = (((0,), (0,)), ((), ()))


def dot(a, b, dims=NN):
    return lax.dot_general(a, b, dims, preferred_element_type=F32)


def one_hot(keys, shape, axis):
    return jnp.where(keys == lax.broadcasted_iota(I32, shape, axis), F32(1), F32(0)).astype(BF16)


def hub_column(hub):
    shape = (8, 8)
    diagonal = lax.broadcasted_iota(I32, shape, 0) == lax.broadcasted_iota(I32, shape, 1)
    spread = jnp.where(diagonal, jnp.broadcast_to(hub, shape), 0).astype(F32)
    return jnp.sum(spread, axis=1, keepdims=True).astype(I32)


def pack_kernel(features, lists, hub, packed, hot, rows):
    by_peer = lists[...].astype(F32).T.astype(I32)
    for slot in range(8):
        hot[slot * PEERS : (slot + 1) * PEERS, :] = one_hot(
            by_peer[:, slot : slot + 1], (PEERS, NODES), 1
        )
    hub_rows = one_hot(hub_column(hub[...]), (8, NODES), 1)
    hot[8 * PEERS : 8 * PEERS + 16, :] = jnp.concatenate(
        [hub_rows, jnp.zeros((8, NODES), BF16)], axis=0
    )
    picked = dot(hot[...], features[...])
    for slot in range(8):
        block = picked[slot * PEERS : (slot + 1) * PEERS]
        rows[0, pl.ds(slot, PEERS, stride=8), :] = block[:, :PEERS]
        rows[1, pl.ds(slot, PEERS, stride=8), :] = block[:, PEERS:]
    hubs = jnp.broadcast_to(picked[8 * PEERS : 8 * PEERS + 8][None], (PEERS, 8, WIDTH))
    bound = jnp.concatenate([rows[0], rows[1]], axis=1).reshape(PEERS, 8, WIDTH)
    packed[...] = jnp.concatenate([bound, hubs], axis=1).astype(BF16)


def pack(features, lists, hub):
    return pl.pallas_call(
        pack_kernel,
        out_shape=jax.ShapeDtypeStruct((PEERS, SLOTS, WIDTH), BF16),
        in_specs=[VMEM] * 3,
        out_specs=VMEM,
        scratch_shapes=[
            pltpu.VMEM((8 * PEERS + 16, NODES), BF16),
            pltpu.VMEM((2, 8 * PEERS, PEERS), F32),
        ],
        compiler_params=pltpu.CompilerParams(vmem_limit_bytes=24 << 20),
        cost_estimate=pl.CostEstimate(
            flops=2 * 1040 * NODES * WIDTH, bytes_accessed=2 << 20, transcendentals=0
        ),
        name="pack",
    )(features, lists, hub)


def flatten_lanes(values):
    n = values.shape[1]
    spread = jnp.where(
        lax.broadcasted_iota(I32, (16, 256), 0) == (lax.broadcasted_iota(I32, (16, 256), 1) & 15),
        F32(1),
        F32(0),
    ).astype(BF16)
    tiled = dot(values.astype(BF16), spread, TN).reshape(n // 16, 16, 256)
    shape = (n // 16, 16, 256)
    mine = (lax.broadcasted_iota(I32, shape, 2) >> 4) == lax.broadcasted_iota(I32, shape, 1)
    return jnp.sum(jnp.where(mine, tiled, F32(0)), axis=1)


def count_kernel(neighbours, counts, features, self_weight, table, summed, pre, key_hi, key_lo):
    index = neighbours[...]
    bound = index - NODES
    hub = bound - 8 * PEERS
    index = jnp.where(
        index < NODES,
        index,
        jnp.where(
            hub < 0,
            NODES + ((bound >> 3) << 4) + (bound & 7),
            NODES + ((hub >> 3) << 4) + 8 + (hub & 7),
        ),
    )
    usable = lax.broadcasted_iota(I32, index.shape, 0) < counts[...]
    index = jnp.where(usable, index, 4096)
    lane = lax.broadcasted_iota(I32, (GROUPS, 256), 1)
    key_hi[...] = flatten_lanes((index >> 8).astype(F32)) * 16.0 + (lane >> 4).astype(F32)
    key_lo[...] = flatten_lanes((index & 255).astype(F32))

    def one_group(group, carry):
        rows = lax.broadcasted_iota(I32, (256, 256), 0).astype(F32).astype(BF16)
        hi = jnp.broadcast_to(key_hi[pl.ds(group, 1), :].astype(BF16), (256, 256))
        lo = jnp.broadcast_to(key_lo[pl.ds(group, 1), :].astype(BF16), (256, 256))
        left = jnp.where(hi == rows, BF16(1), BF16(0))
        right = jnp.where(lo == rows, BF16(1), BF16(0))
        block = dot(left, right, NT).astype(BF16)
        table[:, pl.ds(pl.multiple_of(group * 16, 16), 16), :] = block.reshape(16, 16, 256)
        return carry

    lax.fori_loop(0, GROUPS, one_group, 0, unroll=16)

    def one_block(step, carry):
        at = pl.ds(pl.multiple_of(step * 512, 512), 512)
        total = jnp.zeros((512, WIDTH), F32)
        for hi in range(LOCAL):
            total = total + dot(table[hi, at, :], features[hi * 256 : (hi + 1) * 256, :])
        summed[at, :] = total
        pre[at, :] = dot(features[at, :], self_weight[...])
        return carry

    lax.fori_loop(0, NODES // 512, one_block, 0)


def count(neighbours, counts, features, self_weight):
    return pl.pallas_call(
        count_kernel,
        out_shape=(
            pltpu.VMEM((LOCAL + REMOTE, NODES, WIDTH), BF16),
            pltpu.VMEM((NODES, WIDTH), F32),
            pltpu.VMEM((NODES, WIDTH), F32),
        ),
        in_specs=[VMEM] * 4,
        out_specs=[VMEM] * 3,
        scratch_shapes=[pltpu.VMEM((GROUPS, 256), F32)] * 2,
        compiler_params=pltpu.CompilerParams(vmem_limit_bytes=12 << 20),
        cost_estimate=pl.CostEstimate(
            flops=2 * NODES * 4096 * WIDTH * 2, bytes_accessed=2 << 20, transcendentals=0
        ),
        name="count",
    )(neighbours, counts, features, self_weight)


def node_kernel(
    arrived,
    table,
    summed,
    pre_self,
    features,
    counts,
    cotangent,
    neighbour_weight,
    activations,
    grad_pre,
    edge,
    message,
    mean,
    weights,
    parts,
):
    inverse = (1.0 / counts[...].astype(F32)).T
    remote = arrived[...].reshape(NODES, WIDTH)
    for block in range(NODES // 256):
        at = slice(block * 256, (block + 1) * 256)
        total = summed[at, :]
        for hi in range(REMOTE):
            total = total + dot(table[LOCAL + hi, at, :], remote[hi * 256 : (hi + 1) * 256])
        scale = jnp.concatenate(
            [
                jnp.broadcast_to(inverse[:, 2 * block + half : 2 * block + half + 1], (128, 256))
                for half in range(2)
            ],
            axis=0,
        )
        block_mean = (total * scale).astype(BF16)
        mean[at, :] = block_mean
        pre = pre_self[at, :] + dot(block_mean, neighbour_weight[...])
        sigmoid = 1.0 / (1.0 + jnp.exp(-pre))
        activations[at, :] = (pre * sigmoid).astype(BF16)
        slope = sigmoid * (1.0 + pre * (1.0 - sigmoid))
        block_grad = (cotangent[at, :].astype(F32) * slope).astype(BF16)
        grad_pre[at, :] = block_grad
        edge[at, :] = (dot(block_grad, neighbour_weight[...], NT) * scale).astype(BF16)
    for hi in range(REMOTE):
        added = dot(table[LOCAL + hi], edge[...], TN).astype(BF16).reshape(16, 16, WIDTH)
        message[hi * 16 : (hi + 1) * 16, 0:16, :] = added[:, :, :128]
        message[hi * 16 : (hi + 1) * 16, 16:32, :] = added[:, :, 128:]
    for part, rows in ((0, features), (1, mean)):
        block = dot(rows[...], grad_pre[...], TN)
        weights[0, part * WIDTH : (part + 1) * WIDTH, :] = block[:, :128]
        weights[1, part * WIDTH : (part + 1) * WIDTH, :] = block[:, 128:]
    for half in range(2):
        for row in range(4):
            value = weights[half, pl.ds(row, PEERS, stride=4), :]
            high = value.astype(BF16).astype(F32)
            parts[pl.ds(half * 4 + row, PEERS, stride=16), :] = high
            parts[pl.ds(8 + half * 4 + row, PEERS, stride=16), :] = value - high
    message[:, 32:48, :] = parts[...].astype(BF16).reshape(PEERS, 16, 128)


def node(arrived, table, summed, pre_self, features, counts, cotangent, neighbour_weight):
    return pl.pallas_call(
        node_kernel,
        out_shape=(
            jax.ShapeDtypeStruct((NODES, WIDTH), BF16),
            pltpu.VMEM((NODES, WIDTH), BF16),
            pltpu.VMEM((NODES, WIDTH), BF16),
            jax.ShapeDtypeStruct((PEERS, 48, 128), BF16),
        ),
        in_specs=[VMEM] * 8,
        out_specs=[VMEM] * 4,
        scratch_shapes=[
            pltpu.VMEM((NODES, WIDTH), BF16),
            pltpu.VMEM((2, 2 * WIDTH, 128), F32),
            pltpu.VMEM((NODES, 128), F32),
        ],
        compiler_params=pltpu.CompilerParams(vmem_limit_bytes=20 << 20),
        cost_estimate=pl.CostEstimate(
            flops=2 * NODES * 2048 * WIDTH * 2, bytes_accessed=6 << 20, transcendentals=0
        ),
        name="node",
    )(arrived, table, summed, pre_self, features, counts, cotangent, neighbour_weight)


def local_kernel(table, edge, grad_pre, self_weight, lists, hub, grads, hot, ids):
    for hi in range(LOCAL):
        at = slice(hi * 256, (hi + 1) * 256)
        grads[at, :] = dot(table[hi], edge[...], TN) + dot(grad_pre[at, :], self_weight[...], NT)
    slots = jnp.concatenate(
        [lists[...], jnp.broadcast_to(hub_column(hub[...]), (8, PEERS))], axis=0
    )
    ids[...] = flatten_lanes((slots >> 8).astype(F32)) * 256.0 + flatten_lanes(
        (slots & 255).astype(F32)
    )
    for chunk in range(8):
        row = jnp.broadcast_to(ids[chunk : chunk + 1, :].astype(I32), (NODES, 256))
        hot[:, chunk * 256 : (chunk + 1) * 256] = one_hot(row, (NODES, 256), 0)


def local(table, edge, grad_pre, self_weight, lists, hub):
    return pl.pallas_call(
        local_kernel,
        out_shape=(
            pltpu.VMEM((NODES, WIDTH), F32),
            pltpu.VMEM((NODES, PEERS * SLOTS), BF16),
        ),
        in_specs=[VMEM] * 6,
        out_specs=[VMEM] * 2,
        scratch_shapes=[pltpu.VMEM((8, 256), F32)],
        compiler_params=pltpu.CompilerParams(vmem_limit_bytes=12 << 20),
        cost_estimate=pl.CostEstimate(
            flops=2 * NODES * 2048 * WIDTH, bytes_accessed=2 << 20, transcendentals=0
        ),
        name="local",
    )(table, edge, grad_pre, self_weight, lists, hub)


def finish_kernel(returned, grads, hot, grad_features, grad_weights):
    back = jnp.concatenate([returned[:, 0:16, :], returned[:, 16:32, :]], axis=2)
    back = back.reshape(PEERS * SLOTS, WIDTH)
    grad_features[...] = grads[...] + dot(hot[...], back)
    parts = jnp.sum(returned[:, 32:48, :].astype(F32), axis=0)
    total = parts[:8] + parts[8:]
    grad_weights[...] = jnp.concatenate([total[:4], total[4:]], axis=1)


def finish(returned, grads, hot):
    return pl.pallas_call(
        finish_kernel,
        out_shape=(
            jax.ShapeDtypeStruct((NODES, WIDTH), F32),
            jax.ShapeDtypeStruct((4, WIDTH), F32),
        ),
        in_specs=[VMEM] * 3,
        out_specs=[VMEM] * 2,
        compiler_params=pltpu.CompilerParams(vmem_limit_bytes=16 << 20),
        cost_estimate=pl.CostEstimate(
            flops=2 * NODES * 2048 * WIDTH, bytes_accessed=4 << 20, transcendentals=0
        ),
        name="finish",
    )(returned, grads, hot)


def body(
    features, self_weight, neighbour_weight, send_lists, hub_nodes, neighbours, counts, cotangent
):
    lists = send_lists[0].T
    packed = pack(features, lists, hub_nodes)
    arrived = lax.all_to_all(packed, "dom", split_axis=0, concat_axis=0, tiled=True)
    table, summed, pre_self = count(
        neighbours.T, counts.reshape(1, NODES), features, self_weight
    )
    activations, grad_pre, edge, message = node(
        arrived,
        table,
        summed,
        pre_self,
        features,
        counts.reshape(16, 128),
        cotangent,
        neighbour_weight,
    )
    returned = lax.all_to_all(message, "dom", split_axis=0, concat_axis=0, tiled=True)
    grads, hot = local(table, edge, grad_pre, self_weight, lists, hub_nodes)
    grad_features, grad_weights = finish(returned, grads, hot)
    return (activations, grad_features, grad_weights)


def solution(mesh):
    in_specs = (
        P("dom", None),
        P(),
        P(),
        P("dom", None, None),
        P("dom", None),
        P("dom", None),
        P("dom"),
        P("dom", None),
    )
    out_specs = (P("dom", None), P("dom", None), P("dom", None))
    return jax.shard_map(body, mesh=mesh, in_specs=in_specs, out_specs=out_specs, check_vma=False)
```

```python
import jax
import jax.numpy as jnp
from jax import lax
from jax.experimental import pallas as pl
from jax.experimental.pallas import tpu as pltpu
from jax.sharding import PartitionSpec as P

BF16 = jnp.bfloat16
F32 = jnp.float32
I32 = jnp.int32
NODES = 2048
WIDTH = 256
PEERS = 128
SLOTS = 16
FAN = 16
GROUPS = NODES // 16
LOCAL = 8
REMOTE = 8
VMEM = pl.BlockSpec(memory_space=pltpu.VMEM)
HBM = pl.BlockSpec(memory_space=pltpu.HBM)
DMA = pltpu.SemaphoreType.DMA
BLOCK = 256
BLOCKS = NODES // BLOCK
MESSAGE = 40
STEP = 512
STEPS = NODES // STEP
PIECE = 4
FINISH_PIECE = 4
NN = (((1,), (0,)), ((), ()))
NT = (((1,), (1,)), ((), ()))
TN = (((0,), (0,)), ((), ()))


def dot(a, b, dims=NN):
    return lax.dot_general(a, b, dims, preferred_element_type=F32)


def one_hot(keys, shape, axis):
    return jnp.where(keys == lax.broadcasted_iota(I32, shape, axis), F32(1), F32(0)).astype(BF16)


def hub_column(hub):
    shape = (8, 8)
    diagonal = lax.broadcasted_iota(I32, shape, 0) == lax.broadcasted_iota(I32, shape, 1)
    spread = jnp.where(diagonal, jnp.broadcast_to(hub, shape), 0).astype(F32)
    return jnp.sum(spread, axis=1, keepdims=True).astype(I32)


def in_hbm(*arrays):
    return [pltpu.with_memory_space_constraint(array, pltpu.HBM) for array in arrays]


def start(source, target, semaphore):
    copy = pltpu.make_async_copy(source, target, semaphore)
    copy.start()
    return copy


def rows_of(block):
    return pl.ds(block * BLOCK, BLOCK)


def pack_kernel(features_hbm, lists_hbm, hub_hbm, packed, features, lists, hub, hot, rows, sems):
    get_lists = start(lists_hbm, lists, sems.at[0])
    get_hub = start(hub_hbm, hub, sems.at[1])
    get_features = start(features_hbm, features, sems.at[2])
    get_lists.wait()
    by_peer = lists[...].astype(F32).T.astype(I32)
    for slot in range(8):
        hot[slot * PEERS : (slot + 1) * PEERS, :] = one_hot(
            by_peer[:, slot : slot + 1], (PEERS, NODES), 1
        )
    get_hub.wait()
    hub_rows = one_hot(hub_column(hub[...]), (8, NODES), 1)
    hot[8 * PEERS : 8 * PEERS + 16, :] = jnp.concatenate(
        [hub_rows, jnp.zeros((8, NODES), BF16)], axis=0
    )
    get_features.wait()
    picked = dot(hot[...], features[...])
    for slot in range(8):
        block = picked[slot * PEERS : (slot + 1) * PEERS]
        rows[0, pl.ds(slot, PEERS, stride=8), :] = block[:, :PEERS]
        rows[1, pl.ds(slot, PEERS, stride=8), :] = block[:, PEERS:]
    hubs = jnp.broadcast_to(picked[8 * PEERS : 8 * PEERS + 8][None], (PEERS, 8, WIDTH))
    bound = jnp.concatenate([rows[0], rows[1]], axis=1).reshape(PEERS, 8, WIDTH)
    packed[...] = jnp.concatenate([bound, hubs], axis=1).astype(BF16)


def pack(features, lists, hub):
    return pl.pallas_call(
        pack_kernel,
        out_shape=pltpu.HBM((PEERS, SLOTS, WIDTH), BF16),
        in_specs=[HBM] * 3,
        out_specs=VMEM,
        scratch_shapes=[
            pltpu.VMEM((NODES, WIDTH), BF16),
            pltpu.VMEM((8, PEERS), I32),
            pltpu.VMEM((1, 8), I32),
            pltpu.VMEM((8 * PEERS + 16, NODES), BF16),
            pltpu.VMEM((2, 8 * PEERS, PEERS), F32),
            DMA((3,)),
        ],
        compiler_params=pltpu.CompilerParams(vmem_limit_bytes=24 << 20),
        cost_estimate=pl.CostEstimate(
            flops=2 * 1040 * NODES * WIDTH, bytes_accessed=2 << 20, transcendentals=0
        ),
        name="pack",
    )(*in_hbm(features, lists, hub))


def flatten_lanes(values):
    k, n = values.shape
    per = 256 // k
    lane = lax.broadcasted_iota(I32, (k, 256), 1)
    own = lax.broadcasted_iota(I32, (k, 256), 0) == (lane & (k - 1))
    tiled = dot(values.astype(BF16), jnp.where(own, F32(1), F32(0)).astype(BF16), TN)
    shape = (n // per, per, 256)
    shift = k.bit_length() - 1
    mine = (lax.broadcasted_iota(I32, shape, 2) >> shift) == lax.broadcasted_iota(I32, shape, 1)
    return jnp.sum(jnp.where(mine, tiled.reshape(shape), F32(0)), axis=1)


CHUNK = 512
CHUNKS = NODES // CHUNK


def count_kernel(
    neighbours_hbm,
    counts_hbm,
    features_hbm,
    table_hbm,
    summed_hbm,
    neighbours,
    counts,
    features,
    table,
    summed,
    key_hi,
    key_lo,
    in_sems,
    table_sems,
    summed_sems,
):
    get_neighbours = start(neighbours_hbm, neighbours, in_sems.at[0])
    get_counts = start(counts_hbm, counts, in_sems.at[1])
    get_features = start(features_hbm, features, in_sems.at[2])
    get_neighbours.wait()
    index = neighbours[...]
    bound = index - NODES
    hub = bound - 8 * PEERS
    index = jnp.where(
        index < NODES,
        index,
        jnp.where(
            hub < 0,
            NODES + ((bound >> 3) << 4) + (bound & 7),
            NODES + ((hub >> 3) << 4) + 8 + (hub & 7),
        ),
    )
    get_counts.wait()
    usable = lax.broadcasted_iota(I32, index.shape, 0) < counts[...]
    index = jnp.where(usable, index, 4096)
    lane = lax.broadcasted_iota(I32, (GROUPS, 256), 1)
    key_hi[...] = flatten_lanes((index >> 8).astype(F32)) * 16.0 + (lane >> 4).astype(F32)
    key_lo[...] = flatten_lanes((index & 255).astype(F32))
    get_features.wait()

    def one_group(group, carry):
        rows = lax.broadcasted_iota(I32, (256, 256), 0).astype(F32).astype(BF16)
        hi = jnp.broadcast_to(key_hi[pl.ds(group, 1), :].astype(BF16), (256, 256))
        lo = jnp.broadcast_to(key_lo[pl.ds(group, 1), :].astype(BF16), (256, 256))
        left = jnp.where(hi == rows, BF16(1), BF16(0))
        right = jnp.where(lo == rows, BF16(1), BF16(0))
        block = dot(left, right, NT).astype(BF16)
        table[:, pl.ds(pl.multiple_of(group * 16, 16), 16), :] = block.reshape(16, 16, 256)
        return carry

    copies = []
    for chunk in range(CHUNKS):
        lax.fori_loop(
            chunk * CHUNK // 16, (chunk + 1) * CHUNK // 16, one_group, 0, unroll=16
        )
        at = pl.ds(chunk * CHUNK, CHUNK)
        copies.append(start(table.at[:, at], table_hbm.at[:, at], table_sems.at[chunk]))
        total = jnp.zeros((CHUNK, WIDTH), F32)
        for hi in range(LOCAL):
            total = total + dot(table[hi, at, :], features[hi * 256 : (hi + 1) * 256, :])
        summed[at, :] = total
        copies.append(start(summed.at[at], summed_hbm.at[at], summed_sems.at[chunk]))
    for copy in copies:
        copy.wait()


def count(neighbours, counts, features):
    return pl.pallas_call(
        count_kernel,
        out_shape=(
            pltpu.HBM((LOCAL + REMOTE, NODES, WIDTH), BF16),
            pltpu.HBM((NODES, WIDTH), F32),
        ),
        in_specs=[HBM] * 3,
        out_specs=[HBM] * 2,
        scratch_shapes=[
            pltpu.VMEM((FAN, NODES), I32),
            pltpu.VMEM((1, NODES), I32),
            pltpu.VMEM((NODES, WIDTH), BF16),
            pltpu.VMEM((LOCAL + REMOTE, NODES, WIDTH), BF16),
            pltpu.VMEM((NODES, WIDTH), F32),
            pltpu.VMEM((GROUPS, 256), F32),
            pltpu.VMEM((GROUPS, 256), F32),
            DMA((3,)),
            DMA((CHUNKS,)),
            DMA((CHUNKS,)),
        ],
        compiler_params=pltpu.CompilerParams(vmem_limit_bytes=40 << 20),
        cost_estimate=pl.CostEstimate(
            flops=2 * NODES * 4096 * WIDTH * 2, bytes_accessed=20 << 20, transcendentals=0
        ),
        name="count",
    )(*in_hbm(neighbours, counts, features))


def node_kernel(
    arrived,
    table_hbm,
    summed_hbm,
    features_hbm,
    counts_hbm,
    cotangent_hbm,
    self_weight_hbm,
    neighbour_weight_hbm,
    activations_hbm,
    grad_pre_hbm,
    edge_hbm,
    message_hbm,
    table,
    summed,
    features,
    counts,
    cotangent,
    self_weight,
    neighbour_weight,
    activations,
    grad_pre,
    edge,
    mean,
    message,
    weights,
    parts,
    small_sems,
    in_sems,
    out_sems,
    message_sems,
):
    get_small = [
        start(counts_hbm, counts, small_sems.at[0]),
        start(self_weight_hbm, self_weight, small_sems.at[1]),
        start(neighbour_weight_hbm, neighbour_weight, small_sems.at[2]),
    ]
    get = []
    for step in range(STEPS):
        at = pl.ds(step * STEP, STEP)
        get.append(
            [
                start(
                    table_hbm.at[pl.ds(LOCAL, REMOTE), at], table.at[:, at], in_sems.at[1, step]
                ),
                start(summed_hbm.at[at], summed.at[at], in_sems.at[2, step]),
                start(features_hbm.at[at], features.at[at], in_sems.at[0, step]),
                start(cotangent_hbm.at[at], cotangent.at[at], in_sems.at[3, step]),
            ]
        )
    for copy in get_small:
        copy.wait()
    inverse = (1.0 / counts[...].astype(F32)).T
    remote = arrived[...].reshape(NODES, WIDTH)
    scales = [
        jnp.concatenate(
            [
                jnp.broadcast_to(inverse[:, part : part + 1], (128, 256))
                for part in range(step * STEP // 128, (step + 1) * STEP // 128)
            ],
            axis=0,
        )
        for step in range(STEPS)
    ]

    def gather(step):
        for copy in get[step]:
            copy.wait()
        at = slice(step * STEP, (step + 1) * STEP)
        total = summed[at, :]
        for hi in range(REMOTE):
            total = total + dot(table[hi, at, :], remote[hi * 256 : (hi + 1) * 256])
        return (total * scales[step]).astype(BF16)

    def update(step, block_mean):
        at = slice(step * STEP, (step + 1) * STEP)
        mean[at, :] = block_mean
        pre = dot(features[at, :], self_weight[...]) + dot(block_mean, neighbour_weight[...])
        sigmoid = 0.5 * jnp.tanh(0.5 * pre) + 0.5
        activations[at, :] = (pre * sigmoid).astype(BF16)
        slope = sigmoid * (1.0 + pre * (1.0 - sigmoid))
        block_grad = (cotangent[at, :].astype(F32) * slope).astype(BF16)
        grad_pre[at, :] = block_grad
        edge[at, :] = (dot(block_grad, neighbour_weight[...], NT) * scales[step]).astype(BF16)

    now = gather(0)
    for step in range(STEPS):
        later = gather(step + 1) if step + 1 < STEPS else None
        update(step, now)
        now = later
    put = [
        start(activations, activations_hbm, out_sems.at[0]),
        start(grad_pre, grad_pre_hbm, out_sems.at[1]),
        start(edge, edge_hbm, out_sems.at[2]),
    ]
    for part, left in ((0, features), (1, mean)):
        product = dot(left[...], grad_pre[...], TN)
        weights[0, part * WIDTH : (part + 1) * WIDTH, :] = product[:, :128]
        weights[1, part * WIDTH : (part + 1) * WIDTH, :] = product[:, 128:]
    for half in range(2):
        for row in range(4):
            parts[pl.ds(half * 4 + row, PEERS, stride=8), :] = weights[
                half, pl.ds(row, PEERS, stride=4), :
            ]
    message[:, 32:40, :] = parts[...].reshape(PEERS, 8, 128).astype(BF16)
    for hi in range(REMOTE):
        added = dot(table[hi], edge[...], TN).astype(BF16).reshape(16, 16, WIDTH)
        message[hi * 16 : (hi + 1) * 16, 0:16, :] = added[:, :, :128]
        message[hi * 16 : (hi + 1) * 16, 16:32, :] = added[:, :, 128:]
        if (hi + 1) % PIECE == 0:
            peers = pl.ds((hi + 1 - PIECE) * 16, PIECE * 16)
            put.append(start(message.at[peers], message_hbm.at[peers], message_sems.at[hi]))
    for copy in put:
        copy.wait()


def node(
    arrived, table, summed, features, counts, cotangent, self_weight, neighbour_weight
):
    rows = pltpu.VMEM((NODES, WIDTH), BF16)
    return pl.pallas_call(
        node_kernel,
        out_shape=(
            pltpu.HBM((NODES, WIDTH), BF16),
            pltpu.HBM((NODES, WIDTH), BF16),
            pltpu.HBM((NODES, WIDTH), BF16),
            pltpu.HBM((PEERS, MESSAGE, 128), BF16),
        ),
        in_specs=[VMEM] + [HBM] * 7,
        out_specs=[HBM] * 4,
        scratch_shapes=[
            pltpu.VMEM((REMOTE, NODES, WIDTH), BF16),
            pltpu.VMEM((NODES, WIDTH), F32),
            rows,
            pltpu.VMEM((16, 128), I32),
            rows,
            pltpu.VMEM((WIDTH, WIDTH), BF16),
            pltpu.VMEM((WIDTH, WIDTH), BF16),
            rows,
            rows,
            rows,
            rows,
            pltpu.VMEM((PEERS, MESSAGE, 128), BF16),
            pltpu.VMEM((2, 2 * WIDTH, 128), F32),
            pltpu.VMEM((8 * PEERS, 128), F32),
            DMA((3,)),
            DMA((4, STEPS)),
            DMA((3,)),
            DMA((REMOTE,)),
        ],
        compiler_params=pltpu.CompilerParams(vmem_limit_bytes=40 << 20),
        cost_estimate=pl.CostEstimate(
            flops=2 * NODES * 2048 * WIDTH * 2, bytes_accessed=16 << 20, transcendentals=0
        ),
        name="node",
    )(
        arrived,
        *in_hbm(table, summed, features, counts, cotangent, self_weight, neighbour_weight),
    )


def local_kernel(
    table_hbm,
    edge_hbm,
    grad_pre_hbm,
    self_weight_hbm,
    lists_hbm,
    grads_hbm,
    ids,
    table,
    edge,
    grad_pre,
    self_weight,
    lists,
    grads,
    in_sems,
    table_sems,
    out_sems,
):
    get_edge = start(edge_hbm, edge, in_sems.at[0])
    get = [start(table_hbm.at[hi], table.at[hi], table_sems.at[hi]) for hi in range(LOCAL)]
    get_small = [
        start(grad_pre_hbm, grad_pre, in_sems.at[1]),
        start(self_weight_hbm, self_weight, in_sems.at[2]),
        start(lists_hbm, lists, in_sems.at[3]),
    ]
    for copy in get_small:
        copy.wait()
    ids[...] = flatten_lanes((lists[...] >> 8).astype(F32)) * 256.0 + flatten_lanes(
        (lists[...] & 255).astype(F32)
    )
    get_edge.wait()
    for copy in get:
        copy.wait()
    for hi in range(LOCAL):
        at = slice(hi * 256, (hi + 1) * 256)
        grads[at, :] = dot(table[hi], edge[...], TN) + dot(grad_pre[at, :], self_weight[...], NT)
    start(grads, grads_hbm, out_sems.at[0]).wait()


def local(table, edge, grad_pre, self_weight, lists):
    rows = pltpu.VMEM((NODES, WIDTH), BF16)
    return pl.pallas_call(
        local_kernel,
        out_shape=(
            pltpu.HBM((NODES, WIDTH), F32),
            pltpu.HBM((4, 256), F32),
        ),
        in_specs=[HBM] * 5,
        out_specs=[HBM, VMEM],
        scratch_shapes=[
            pltpu.VMEM((LOCAL, NODES, WIDTH), BF16),
            rows,
            rows,
            pltpu.VMEM((WIDTH, WIDTH), BF16),
            pltpu.VMEM((8, PEERS), I32),
            pltpu.VMEM((NODES, WIDTH), F32),
            DMA((4,)),
            DMA((LOCAL,)),
            DMA((1,)),
        ],
        compiler_params=pltpu.CompilerParams(vmem_limit_bytes=40 << 20),
        cost_estimate=pl.CostEstimate(
            flops=2 * NODES * 2048 * WIDTH, bytes_accessed=14 << 20, transcendentals=0
        ),
        name="local",
    )(*in_hbm(table, edge, grad_pre, self_weight, lists))


def finish_kernel(
    returned,
    grads_hbm,
    ids_hbm,
    hub_hbm,
    grad_features_hbm,
    grad_weights,
    grads,
    ids,
    hub,
    totals,
    sems,
    put_sems,
):
    get_ids = start(ids_hbm, ids, sems.at[0])
    get_hub = start(hub_hbm, hub, sems.at[1])
    get_grads = start(grads_hbm, grads, sems.at[2])
    sides = [returned[:, 0:16, :].astype(F32), returned[:, 16:32, :].astype(F32)]
    bound = jnp.concatenate([side[:, :8].reshape(8 * PEERS, 128) for side in sides], axis=1)
    bound = bound.astype(BF16)
    hubs = jnp.concatenate([jnp.sum(side[:, 8:], axis=0) for side in sides], axis=1)
    high = hubs.astype(BF16).astype(F32)
    hubs = jnp.concatenate([high, hubs - high], axis=0).astype(BF16)
    weights = jnp.sum(returned[:, 32:40, :].astype(F32), axis=0)
    grad_weights[...] = jnp.concatenate([weights[:4], weights[4:]], axis=1)
    get_ids.wait()
    get_hub.wait()
    get_grads.wait()
    put = []
    rows = lax.broadcasted_iota(I32, (BLOCK, 256), 0).astype(F32).astype(BF16)
    twice = jnp.concatenate([hub[...], hub[...]], axis=1)
    for block in range(BLOCKS):
        at = slice(block * BLOCK, (block + 1) * BLOCK)
        offset = ids[...] - block * 256.0
        inside = (offset >= 0.0) & (offset < 256.0)
        keys = jnp.where(inside, offset, -1.0).astype(BF16)
        hot = jnp.concatenate(
            [
                jnp.where(
                    jnp.broadcast_to(keys[part : part + 1, :], (BLOCK, 256)) == rows,
                    BF16(1),
                    BF16(0),
                )
                for part in range(4)
            ],
            axis=1,
        )
        hub_hot = one_hot(
            jnp.broadcast_to(twice - block * BLOCK, (BLOCK, 16)), (BLOCK, 16), 0
        )
        totals[at, :] = grads[at, :] + dot(hot, bound) + dot(hub_hot, hubs)
        if (block + 1) % FINISH_PIECE == 0:
            piece = pl.ds((block + 1 - FINISH_PIECE) * BLOCK, FINISH_PIECE * BLOCK)
            put.append(start(totals.at[piece], grad_features_hbm.at[piece], put_sems.at[block]))
    for copy in put:
        copy.wait()


def finish(returned, grads, ids, hub):
    return pl.pallas_call(
        finish_kernel,
        out_shape=(
            pltpu.HBM((NODES, WIDTH), F32),
            jax.ShapeDtypeStruct((4, WIDTH), F32),
        ),
        in_specs=[VMEM, HBM, HBM, HBM],
        out_specs=[HBM, VMEM],
        scratch_shapes=[
            pltpu.VMEM((NODES, WIDTH), F32),
            pltpu.VMEM((4, 256), F32),
            pltpu.VMEM((1, 8), I32),
            pltpu.VMEM((NODES, WIDTH), F32),
            DMA((3,)),
            DMA((BLOCKS,)),
        ],
        compiler_params=pltpu.CompilerParams(vmem_limit_bytes=32 << 20),
        cost_estimate=pl.CostEstimate(
            flops=2 * NODES * 1024 * WIDTH, bytes_accessed=6 << 20, transcendentals=0
        ),
        name="finish",
    )(returned, *in_hbm(grads, ids, hub))


def body(
    features, self_weight, neighbour_weight, send_lists, hub_nodes, neighbours, counts, cotangent
):
    lists = send_lists[0].T
    packed = pack(features, lists, hub_nodes)
    arrived = lax.all_to_all(packed, "dom", split_axis=0, concat_axis=0, tiled=True)
    table, summed = count(neighbours.T, counts.reshape(1, NODES), features)
    activations, grad_pre, edge, message = node(
        arrived,
        table,
        summed,
        features,
        counts.reshape(16, 128),
        cotangent,
        self_weight,
        neighbour_weight,
    )
    returned = lax.all_to_all(message, "dom", split_axis=0, concat_axis=0, tiled=True)
    grads, ids = local(table, edge, grad_pre, self_weight, lists)
    grad_features, grad_weights = finish(returned, grads, ids, hub_nodes)
    return (activations, grad_features, grad_weights)


def solution(mesh):
    in_specs = (
        P("dom", None),
        P(),
        P(),
        P("dom", None, None),
        P("dom", None),
        P("dom", None),
        P("dom"),
        P("dom", None),
    )
    out_specs = (P("dom", None), P("dom", None), P("dom", None))
    return jax.shard_map(body, mesh=mesh, in_specs=in_specs, out_specs=out_specs, check_vma=False)
```

```python
import jax
import jax.numpy as jnp
from jax import lax
from jax.experimental import pallas as pl
from jax.experimental.pallas import tpu as pltpu
from jax.sharding import PartitionSpec as P

BF16 = jnp.bfloat16
COUNT = jnp.float8_e4m3fn
PRODUCT = jnp.float8_e4m3fn
UNROLL = 16
F32 = jnp.float32
I32 = jnp.int32
NODES = 2048
WIDTH = 256
PEERS = 128
SLOTS = 16
FAN = 16
GROUPS = NODES // 16
LOCAL = 8
REMOTE = 8
VMEM = pl.BlockSpec(memory_space=pltpu.VMEM)
HBM = pl.BlockSpec(memory_space=pltpu.HBM)
DMA = pltpu.SemaphoreType.DMA
BLOCK = 256
BLOCKS = NODES // BLOCK
MESSAGE = 40
STEP = 512
STEPS = NODES // STEP
PIECE = 4
FINISH_PIECE = 2
NN = (((1,), (0,)), ((), ()))
NT = (((1,), (1,)), ((), ()))
TN = (((0,), (0,)), ((), ()))


def dot(a, b, dims=NN):
    return lax.dot_general(a, b, dims, preferred_element_type=F32)


def one_hot(keys, shape, axis):
    return jnp.where(keys == lax.broadcasted_iota(I32, shape, axis), F32(1), F32(0)).astype(BF16)


def hub_column(hub):
    shape = (8, 8)
    diagonal = lax.broadcasted_iota(I32, shape, 0) == lax.broadcasted_iota(I32, shape, 1)
    spread = jnp.where(diagonal, jnp.broadcast_to(hub, shape), 0).astype(F32)
    return jnp.sum(spread, axis=1, keepdims=True).astype(I32)


def in_hbm(*arrays):
    return [pltpu.with_memory_space_constraint(array, pltpu.HBM) for array in arrays]


def start(source, target, semaphore, priority=0):
    copy = pltpu.make_async_copy(source, target, semaphore)
    copy.start(priority=priority)
    return copy


def rows_of(block):
    return pl.ds(block * BLOCK, BLOCK)


def pack_kernel(features_hbm, lists_hbm, hub_hbm, packed, features, lists, hub, rows, sems):
    get_lists = start(lists_hbm, lists, sems.at[0])
    get_hub = start(hub_hbm, hub, sems.at[1])
    get_features = start(features_hbm, features, sems.at[2])
    get_lists.wait()
    get_hub.wait()
    get_features.wait()
    by_peer = lists[...].astype(F32).T.astype(I32)
    none = jnp.full((8, 1), -1, I32)
    column = jnp.concatenate(
        [by_peer[:, slot : slot + 1] for slot in range(8)] + [hub_column(hub[...]), none], axis=0
    )
    shape = (8 * PEERS + 16, 256)
    picked = jnp.zeros(shape, F32)
    for chunk in range(8):
        hot = one_hot(jnp.broadcast_to(column - chunk * 256, shape), shape, 1)
        picked = picked + dot(hot, features[chunk * 256 : (chunk + 1) * 256, :])
    for slot in range(8):
        block = picked[slot * PEERS : (slot + 1) * PEERS]
        rows[0, pl.ds(slot, PEERS, stride=8), :] = block[:, :PEERS]
        rows[1, pl.ds(slot, PEERS, stride=8), :] = block[:, PEERS:]
    hubs = jnp.broadcast_to(picked[8 * PEERS : 8 * PEERS + 8][None], (PEERS, 8, WIDTH))
    bound = jnp.concatenate([rows[0], rows[1]], axis=1).reshape(PEERS, 8, WIDTH)
    packed[...] = jnp.concatenate([bound, hubs], axis=1).astype(BF16)


def pack(features, lists, hub):
    return pl.pallas_call(
        pack_kernel,
        out_shape=pltpu.HBM((PEERS, SLOTS, WIDTH), BF16),
        in_specs=[HBM] * 3,
        out_specs=VMEM,
        scratch_shapes=[
            pltpu.VMEM((NODES, WIDTH), BF16),
            pltpu.VMEM((8, PEERS), I32),
            pltpu.VMEM((1, 8), I32),
            pltpu.VMEM((2, 8 * PEERS, PEERS), F32),
            DMA((3,)),
        ],
        compiler_params=pltpu.CompilerParams(vmem_limit_bytes=24 << 20),
        cost_estimate=pl.CostEstimate(
            flops=2 * 1040 * NODES * WIDTH, bytes_accessed=2 << 20, transcendentals=0
        ),
        name="pack",
    )(*in_hbm(features, lists, hub))


def flatten_lanes(values):
    k, n = values.shape
    per = 256 // k
    lane = lax.broadcasted_iota(I32, (k, 256), 1)
    own = lax.broadcasted_iota(I32, (k, 256), 0) == (lane & (k - 1))
    tiled = dot(values.astype(BF16), jnp.where(own, F32(1), F32(0)).astype(BF16), TN)
    shape = (n // per, per, 256)
    shift = k.bit_length() - 1
    mine = (lax.broadcasted_iota(I32, shape, 2) >> shift) == lax.broadcasted_iota(I32, shape, 1)
    return jnp.sum(jnp.where(mine, tiled.reshape(shape), F32(0)), axis=1)


CHUNK = 512
CHUNKS = NODES // CHUNK


def count_kernel(
    neighbours_hbm,
    counts_hbm,
    features_hbm,
    table_hbm,
    summed_hbm,
    neighbours,
    counts,
    features,
    table,
    summed,
    key_hi,
    key_lo,
    in_sems,
    table_sems,
    summed_sems,
):
    get_neighbours = start(neighbours_hbm, neighbours, in_sems.at[0])
    get_counts = start(counts_hbm, counts, in_sems.at[1])
    get_features = start(features_hbm, features, in_sems.at[2])
    get_neighbours.wait()
    index = neighbours[...]
    bound = index - NODES
    hub = bound - 8 * PEERS
    index = jnp.where(
        index < NODES,
        index,
        jnp.where(
            hub < 0,
            NODES + ((bound >> 3) << 4) + (bound & 7),
            NODES + ((hub >> 3) << 4) + 8 + (hub & 7),
        ),
    )
    get_counts.wait()
    usable = lax.broadcasted_iota(I32, index.shape, 0) < counts[...]
    index = jnp.where(usable, index, 4096)
    lane = lax.broadcasted_iota(I32, (GROUPS, 256), 1)
    key_hi[...] = flatten_lanes((index >> 8).astype(F32)) * 16.0 + (lane >> 4).astype(F32)
    key_lo[...] = flatten_lanes((index & 255).astype(F32))
    get_features.wait()

    rows = lax.broadcasted_iota(I32, (256, 256), 0).astype(F32).astype(BF16)

    def products(group):
        hi = jnp.broadcast_to(key_hi[pl.ds(group, 1), :].astype(BF16), (256, 256))
        lo = jnp.broadcast_to(key_lo[pl.ds(group, 1), :].astype(BF16), (256, 256))
        left = jnp.where(hi == rows, BF16(1), BF16(0)).astype(PRODUCT)
        right = jnp.where(lo == rows, BF16(1), BF16(0)).astype(PRODUCT)
        return dot(left, right, NT).reshape(16, 16, 256)

    def one_pair(pair, carry):
        both = jnp.concatenate([products(2 * pair), products(2 * pair + 1)], axis=1)
        at = pl.ds(pl.multiple_of(pair * 32, 32), 32)
        table[:, at, :] = both.astype(COUNT)
        return carry

    copies = []
    for chunk in range(CHUNKS):
        lax.fori_loop(
            chunk * CHUNK // 32, (chunk + 1) * CHUNK // 32, one_pair, 0, unroll=UNROLL
        )
        at = pl.ds(chunk * CHUNK, CHUNK)
        copies.append(start(table.at[:, at], table_hbm.at[:, at], table_sems.at[chunk]))
    for half in range(2):
        for block in range(2 * half, 2 * half + 2):
            at = slice(block * 512, (block + 1) * 512)
            total = jnp.zeros((512, WIDTH), F32)
            for hi in range(LOCAL):
                total = total + dot(
                    table[hi, at, :].astype(BF16), features[hi * 256 : (hi + 1) * 256, :]
                )
            summed[at, :] = total
        at = pl.ds(half * 1024, 1024)
        copies.append(start(summed.at[at], summed_hbm.at[at], summed_sems.at[half]))
    for copy in copies:
        copy.wait()


def count(neighbours, counts, features):
    return pl.pallas_call(
        count_kernel,
        out_shape=(
            pltpu.HBM((LOCAL + REMOTE, NODES, WIDTH), COUNT),
            pltpu.HBM((NODES, WIDTH), F32),
        ),
        in_specs=[HBM] * 3,
        out_specs=[HBM] * 2,
        scratch_shapes=[
            pltpu.VMEM((FAN, NODES), I32),
            pltpu.VMEM((1, NODES), I32),
            pltpu.VMEM((NODES, WIDTH), BF16),
            pltpu.VMEM((LOCAL + REMOTE, NODES, WIDTH), COUNT),
            pltpu.VMEM((NODES, WIDTH), F32),
            pltpu.VMEM((GROUPS, 256), F32),
            pltpu.VMEM((GROUPS, 256), F32),
            DMA((3,)),
            DMA((CHUNKS,)),
            DMA((CHUNKS,)),
        ],
        compiler_params=pltpu.CompilerParams(vmem_limit_bytes=40 << 20),
        cost_estimate=pl.CostEstimate(
            flops=2 * NODES * 4096 * WIDTH * 2, bytes_accessed=20 << 20, transcendentals=0
        ),
        name="count",
    )(*in_hbm(neighbours, counts, features))


def node_kernel(
    arrived,
    table_hbm,
    summed_hbm,
    features_hbm,
    counts_hbm,
    cotangent_hbm,
    self_weight_hbm,
    neighbour_weight_hbm,
    activations_hbm,
    grad_pre_hbm,
    edge_hbm,
    message_hbm,
    table,
    summed,
    features,
    counts,
    cotangent,
    self_weight,
    neighbour_weight,
    activations,
    grad_pre,
    edge,
    mean,
    message,
    weights,
    parts,
    small_sems,
    in_sems,
    out_sems,
    message_sems,
):
    get_small = [
        start(counts_hbm, counts, small_sems.at[0]),
        start(self_weight_hbm, self_weight, small_sems.at[1]),
        start(neighbour_weight_hbm, neighbour_weight, small_sems.at[2]),
    ]
    get = []
    for step in range(STEPS):
        at = pl.ds(step * STEP, STEP)
        late = min(step, 1)
        get.append(
            [
                start(
                    table_hbm.at[pl.ds(LOCAL, REMOTE), at],
                    table.at[:, at],
                    in_sems.at[1, step],
                    late,
                ),
                start(summed_hbm.at[at], summed.at[at], in_sems.at[2, step], late),
                start(features_hbm.at[at], features.at[at], in_sems.at[0, step], late),
                start(cotangent_hbm.at[at], cotangent.at[at], in_sems.at[3, step], late),
            ]
        )
    for copy in get_small:
        copy.wait()
    inverse = (1.0 / counts[...].astype(F32)).T
    remote = arrived[...].reshape(NODES, WIDTH)
    scales = [
        jnp.concatenate(
            [
                jnp.broadcast_to(inverse[:, part : part + 1], (128, 256))
                for part in range(step * STEP // 128, (step + 1) * STEP // 128)
            ],
            axis=0,
        )
        for step in range(STEPS)
    ]

    def gather(step):
        for copy in get[step]:
            copy.wait()
        at = slice(step * STEP, (step + 1) * STEP)
        total = summed[at, :]
        for hi in range(REMOTE):
            total = total + dot(table[hi, at, :].astype(BF16), remote[hi * 256 : (hi + 1) * 256])
        return (total * scales[step]).astype(BF16)

    def update(step, block_mean):
        at = slice(step * STEP, (step + 1) * STEP)
        mean[at, :] = block_mean
        pre = dot(features[at, :], self_weight[...]) + dot(block_mean, neighbour_weight[...])
        sigmoid = 0.5 * jnp.tanh(0.5 * pre) + 0.5
        activations[at, :] = (pre * sigmoid).astype(BF16)
        slope = sigmoid * (1.0 + pre * (1.0 - sigmoid))
        block_grad = (cotangent[at, :].astype(F32) * slope).astype(BF16)
        grad_pre[at, :] = block_grad
        edge[at, :] = (dot(block_grad, neighbour_weight[...], NT) * scales[step]).astype(BF16)

    now = gather(0)
    for step in range(STEPS):
        later = gather(step + 1) if step + 1 < STEPS else None
        update(step, now)
        now = later
    put = [
        start(activations, activations_hbm, out_sems.at[0]),
        start(grad_pre, grad_pre_hbm, out_sems.at[1]),
        start(edge, edge_hbm, out_sems.at[2]),
    ]
    for part, left in ((0, features), (1, mean)):
        product = dot(left[...], grad_pre[...], TN)
        weights[0, part * WIDTH : (part + 1) * WIDTH, :] = product[:, :128]
        weights[1, part * WIDTH : (part + 1) * WIDTH, :] = product[:, 128:]
    for half in range(2):
        for row in range(4):
            parts[pl.ds(half * 4 + row, PEERS, stride=8), :] = weights[
                half, pl.ds(row, PEERS, stride=4), :
            ]
    message[:, 32:40, :] = parts[...].reshape(PEERS, 8, 128).astype(BF16)
    for hi in range(REMOTE):
        added = dot(table[hi].astype(BF16), edge[...], TN).astype(BF16).reshape(16, 16, WIDTH)
        message[hi * 16 : (hi + 1) * 16, 0:16, :] = added[:, :, :128]
        message[hi * 16 : (hi + 1) * 16, 16:32, :] = added[:, :, 128:]
        if (hi + 1) % PIECE == 0:
            peers = pl.ds((hi + 1 - PIECE) * 16, PIECE * 16)
            put.append(start(message.at[peers], message_hbm.at[peers], message_sems.at[hi]))
    for copy in put:
        copy.wait()


def node(
    arrived, table, summed, features, counts, cotangent, self_weight, neighbour_weight
):
    rows = pltpu.VMEM((NODES, WIDTH), BF16)
    return pl.pallas_call(
        node_kernel,
        out_shape=(
            pltpu.HBM((NODES, WIDTH), BF16),
            pltpu.HBM((NODES, WIDTH), BF16),
            pltpu.HBM((NODES, WIDTH), BF16),
            pltpu.HBM((PEERS, MESSAGE, 128), BF16),
        ),
        in_specs=[VMEM] + [HBM] * 7,
        out_specs=[HBM] * 4,
        scratch_shapes=[
            pltpu.VMEM((REMOTE, NODES, WIDTH), COUNT),
            pltpu.VMEM((NODES, WIDTH), F32),
            rows,
            pltpu.VMEM((16, 128), I32),
            rows,
            pltpu.VMEM((WIDTH, WIDTH), BF16),
            pltpu.VMEM((WIDTH, WIDTH), BF16),
            rows,
            rows,
            rows,
            rows,
            pltpu.VMEM((PEERS, MESSAGE, 128), BF16),
            pltpu.VMEM((2, 2 * WIDTH, 128), F32),
            pltpu.VMEM((8 * PEERS, 128), F32),
            DMA((3,)),
            DMA((4, STEPS)),
            DMA((3,)),
            DMA((REMOTE,)),
        ],
        compiler_params=pltpu.CompilerParams(vmem_limit_bytes=40 << 20),
        cost_estimate=pl.CostEstimate(
            flops=2 * NODES * 2048 * WIDTH * 2, bytes_accessed=16 << 20, transcendentals=0
        ),
        name="node",
    )(
        arrived,
        *in_hbm(table, summed, features, counts, cotangent, self_weight, neighbour_weight),
    )


def local_kernel(
    table_hbm,
    edge_hbm,
    grad_pre_hbm,
    self_weight_hbm,
    lists_hbm,
    grads_hbm,
    ids,
    table,
    edge,
    grad_pre,
    self_weight,
    lists,
    grads,
    in_sems,
    table_sems,
    out_sems,
):
    get_edge = start(edge_hbm, edge, in_sems.at[0])
    get = [start(table_hbm.at[hi], table.at[hi], table_sems.at[hi]) for hi in range(LOCAL)]
    get_small = [
        start(grad_pre_hbm, grad_pre, in_sems.at[1]),
        start(self_weight_hbm, self_weight, in_sems.at[2]),
        start(lists_hbm, lists, in_sems.at[3]),
    ]
    for copy in get_small:
        copy.wait()
    ids[...] = flatten_lanes((lists[...] >> 8).astype(F32)) * 256.0 + flatten_lanes(
        (lists[...] & 255).astype(F32)
    )
    get_edge.wait()
    for copy in get:
        copy.wait()
    for hi in range(LOCAL):
        at = slice(hi * 256, (hi + 1) * 256)
        grads[at, :] = dot(table[hi].astype(BF16), edge[...], TN) + dot(grad_pre[at, :], self_weight[...], NT)
    start(grads, grads_hbm, out_sems.at[0]).wait()


def local(table, edge, grad_pre, self_weight, lists):
    rows = pltpu.VMEM((NODES, WIDTH), BF16)
    return pl.pallas_call(
        local_kernel,
        out_shape=(
            pltpu.HBM((NODES, WIDTH), F32),
            pltpu.HBM((4, 256), F32),
        ),
        in_specs=[HBM] * 5,
        out_specs=[HBM, VMEM],
        scratch_shapes=[
            pltpu.VMEM((LOCAL, NODES, WIDTH), COUNT),
            rows,
            rows,
            pltpu.VMEM((WIDTH, WIDTH), BF16),
            pltpu.VMEM((8, PEERS), I32),
            pltpu.VMEM((NODES, WIDTH), F32),
            DMA((4,)),
            DMA((LOCAL,)),
            DMA((1,)),
        ],
        compiler_params=pltpu.CompilerParams(vmem_limit_bytes=40 << 20),
        cost_estimate=pl.CostEstimate(
            flops=2 * NODES * 2048 * WIDTH, bytes_accessed=14 << 20, transcendentals=0
        ),
        name="local",
    )(*in_hbm(table, edge, grad_pre, self_weight, lists))


def finish_kernel(
    returned,
    grads_hbm,
    ids_hbm,
    hub_hbm,
    grad_features_hbm,
    grad_weights,
    grads,
    ids,
    hub,
    totals,
    sems,
    put_sems,
):
    get_ids = start(ids_hbm, ids, sems.at[0])
    get_hub = start(hub_hbm, hub, sems.at[1])
    get_grads = start(grads_hbm, grads, sems.at[2])
    sides = [returned[:, 0:16, :].astype(F32), returned[:, 16:32, :].astype(F32)]
    bound = jnp.concatenate([side[:, :8].reshape(8 * PEERS, 128) for side in sides], axis=1)
    bound = bound.astype(BF16)
    hubs = jnp.concatenate([jnp.sum(side[:, 8:], axis=0) for side in sides], axis=1)
    high = hubs.astype(BF16).astype(F32)
    hubs = jnp.concatenate([high, hubs - high], axis=0).astype(BF16)
    weights = jnp.sum(returned[:, 32:40, :].astype(F32), axis=0)
    grad_weights[...] = jnp.concatenate([weights[:4], weights[4:]], axis=1)
    get_ids.wait()
    get_hub.wait()
    get_grads.wait()
    put = []
    rows = lax.broadcasted_iota(I32, (BLOCK, 256), 0).astype(F32).astype(BF16)
    twice = jnp.concatenate([hub[...], hub[...]], axis=1)
    for block in range(BLOCKS):
        at = slice(block * BLOCK, (block + 1) * BLOCK)
        offset = ids[...] - block * 256.0
        inside = (offset >= 0.0) & (offset < 256.0)
        keys = jnp.where(inside, offset, -1.0).astype(BF16)
        hot = jnp.concatenate(
            [
                jnp.where(
                    jnp.broadcast_to(keys[part : part + 1, :], (BLOCK, 256)) == rows,
                    BF16(1),
                    BF16(0),
                )
                for part in range(4)
            ],
            axis=1,
        )
        hub_hot = one_hot(
            jnp.broadcast_to(twice - block * BLOCK, (BLOCK, 16)), (BLOCK, 16), 0
        )
        totals[at, :] = grads[at, :] + dot(hot, bound) + dot(hub_hot, hubs)
        if (block + 1) % FINISH_PIECE == 0:
            piece = pl.ds((block + 1 - FINISH_PIECE) * BLOCK, FINISH_PIECE * BLOCK)
            put.append(start(totals.at[piece], grad_features_hbm.at[piece], put_sems.at[block]))
    for copy in put:
        copy.wait()


def finish(returned, grads, ids, hub):
    return pl.pallas_call(
        finish_kernel,
        out_shape=(
            pltpu.HBM((NODES, WIDTH), F32),
            jax.ShapeDtypeStruct((4, WIDTH), F32),
        ),
        in_specs=[VMEM, HBM, HBM, HBM],
        out_specs=[HBM, VMEM],
        scratch_shapes=[
            pltpu.VMEM((NODES, WIDTH), F32),
            pltpu.VMEM((4, 256), F32),
            pltpu.VMEM((1, 8), I32),
            pltpu.VMEM((NODES, WIDTH), F32),
            DMA((3,)),
            DMA((BLOCKS,)),
        ],
        compiler_params=pltpu.CompilerParams(vmem_limit_bytes=32 << 20),
        cost_estimate=pl.CostEstimate(
            flops=2 * NODES * 1024 * WIDTH, bytes_accessed=6 << 20, transcendentals=0
        ),
        name="finish",
    )(returned, *in_hbm(grads, ids, hub))


def body(
    features, self_weight, neighbour_weight, send_lists, hub_nodes, neighbours, counts, cotangent
):
    lists = send_lists[0].T
    packed = pack(features, lists, hub_nodes)
    arrived = lax.all_to_all(packed, "dom", split_axis=0, concat_axis=0, tiled=True)
    table, summed = count(neighbours.T, counts.reshape(1, NODES), features)
    activations, grad_pre, edge, message = node(
        arrived,
        table,
        summed,
        features,
        counts.reshape(16, 128),
        cotangent,
        self_weight,
        neighbour_weight,
    )
    returned = lax.all_to_all(message, "dom", split_axis=0, concat_axis=0, tiled=True)
    grads, ids = local(table, edge, grad_pre, self_weight, lists)
    grad_features, grad_weights = finish(returned, grads, ids, hub_nodes)
    return (activations, grad_features, grad_weights)


def solution(mesh):
    in_specs = (
        P("dom", None),
        P(),
        P(),
        P("dom", None, None),
        P("dom", None),
        P("dom", None),
        P("dom"),
        P("dom", None),
    )
    out_specs = (P("dom", None), P("dom", None), P("dom", None))
    return jax.shard_map(body, mesh=mesh, in_specs=in_specs, out_specs=out_specs, check_vma=False)
```

```python
import jax
import jax.numpy as jnp
from jax import lax
from jax.experimental import pallas as pl
from jax.experimental.pallas import tpu as pltpu
from jax.sharding import PartitionSpec as P

BF16 = jnp.bfloat16
COUNT = jnp.float8_e4m3fn
PRODUCT = jnp.float8_e4m3fn
UNROLL = 16
F32 = jnp.float32
I32 = jnp.int32
NODES = 2048
WIDTH = 256
PEERS = 128
SLOTS = 16
FAN = 16
GROUPS = NODES // 16
LOCAL = 8
REMOTE = 8
VMEM = pl.BlockSpec(memory_space=pltpu.VMEM)
HBM = pl.BlockSpec(memory_space=pltpu.HBM)
DMA = pltpu.SemaphoreType.DMA
BLOCK = 256
BLOCKS = NODES // BLOCK
MESSAGE = 40
CUTS = (0, 256, 768, 1280, 2048)
STEPS = len(CUTS) - 1
PIECE = 4
FINISH_PIECE = 2
NN = (((1,), (0,)), ((), ()))
NT = (((1,), (1,)), ((), ()))
TN = (((0,), (0,)), ((), ()))


def dot(a, b, dims=NN):
    return lax.dot_general(a, b, dims, preferred_element_type=F32)


def one_hot(keys, shape, axis):
    return jnp.where(keys == lax.broadcasted_iota(I32, shape, axis), F32(1), F32(0)).astype(BF16)


def in_hbm(*arrays):
    return [pltpu.with_memory_space_constraint(array, pltpu.HBM) for array in arrays]


def start(source, target, semaphore, priority=0):
    copy = pltpu.make_async_copy(source, target, semaphore)
    copy.start(priority=priority)
    return copy


def rows_of(block):
    return pl.ds(block * BLOCK, BLOCK)


def flatten_lanes(values):
    k, n = values.shape
    per = 256 // k
    lane = lax.broadcasted_iota(I32, (k, 256), 1)
    own = lax.broadcasted_iota(I32, (k, 256), 0) == (lane & (k - 1))
    tiled = dot(values.astype(BF16), jnp.where(own, F32(1), F32(0)).astype(BF16), TN)
    shape = (n // per, per, 256)
    shift = k.bit_length() - 1
    mine = (lax.broadcasted_iota(I32, shape, 2) >> shift) == lax.broadcasted_iota(I32, shape, 1)
    return jnp.sum(jnp.where(mine, tiled.reshape(shape), F32(0)), axis=1)


def pack_kernel(features_hbm, lists_hbm, hub_hbm, packed, features, lists, hub, sems):
    get_lists = start(lists_hbm, lists, sems.at[0])
    get_hub = start(hub_hbm, hub, sems.at[1])
    get_features = start(features_hbm, features, sems.at[2])
    get_lists.wait()
    get_hub.wait()
    get_features.wait()
    ids = flatten_lanes((lists[...] >> 8).astype(F32)) * 256.0 + flatten_lanes(
        (lists[...] & 255).astype(F32)
    )
    hub_ids = jnp.concatenate([hub[...].astype(F32), jnp.full((1, 120), -1.0, F32)], axis=1)
    ids = jnp.concatenate([ids[part : part + 1] for part in range(4)] + [hub_ids], axis=1)
    rows = lax.broadcasted_iota(I32, (256, 1152), 0).astype(F32).astype(BF16)
    picked = jnp.zeros((1152, WIDTH), F32)
    for chunk in range(8):
        offset = ids - chunk * 256.0
        inside = (offset >= 0.0) & (offset < 256.0)
        keys = jnp.where(inside, offset, -1.0).astype(BF16)
        hot = jnp.where(jnp.broadcast_to(keys, (256, 1152)) == rows, BF16(1), BF16(0))
        picked = picked + dot(hot, features[chunk * 256 : (chunk + 1) * 256, :], TN)
    hubs = jnp.broadcast_to(picked[8 * PEERS : 8 * PEERS + 8][None], (PEERS, 8, WIDTH))
    bound = picked[: 8 * PEERS].reshape(PEERS, 8, WIDTH)
    packed[...] = jnp.concatenate([bound, hubs], axis=1).astype(BF16)


def pack(features, lists, hub):
    return pl.pallas_call(
        pack_kernel,
        out_shape=pltpu.HBM((PEERS, SLOTS, WIDTH), BF16),
        in_specs=[HBM] * 3,
        out_specs=VMEM,
        scratch_shapes=[
            pltpu.VMEM((NODES, WIDTH), BF16),
            pltpu.VMEM((8, PEERS), I32),
            pltpu.VMEM((1, 8), I32),
            DMA((3,)),
        ],
        compiler_params=pltpu.CompilerParams(vmem_limit_bytes=24 << 20),
        cost_estimate=pl.CostEstimate(
            flops=2 * 1040 * NODES * WIDTH, bytes_accessed=2 << 20, transcendentals=0
        ),
        name="pack",
    )(*in_hbm(features, lists, hub))


CHUNK = 512
CHUNKS = NODES // CHUNK


def count_kernel(
    neighbours_hbm,
    counts_hbm,
    features_hbm,
    table_hbm,
    summed_hbm,
    neighbours,
    counts,
    features,
    table,
    summed,
    key_hi,
    key_lo,
    in_sems,
    table_sems,
    summed_sems,
):
    get_neighbours = start(neighbours_hbm, neighbours, in_sems.at[0])
    get_counts = start(counts_hbm, counts, in_sems.at[1])
    get_features = start(features_hbm, features, in_sems.at[2])
    get_neighbours.wait()
    index = neighbours[...]
    bound = index - NODES
    hub = bound - 8 * PEERS
    index = jnp.where(
        index < NODES,
        index,
        jnp.where(
            hub < 0,
            NODES + ((bound >> 3) << 4) + (bound & 7),
            NODES + ((hub >> 3) << 4) + 8 + (hub & 7),
        ),
    )
    get_counts.wait()
    usable = lax.broadcasted_iota(I32, index.shape, 0) < counts[...]
    index = jnp.where(usable, index, 4096)
    lane = lax.broadcasted_iota(I32, (GROUPS, 256), 1)
    key_hi[...] = flatten_lanes((index >> 8).astype(F32)) * 16.0 + (lane >> 4).astype(F32)
    key_lo[...] = flatten_lanes((index & 255).astype(F32))
    get_features.wait()

    rows = lax.broadcasted_iota(I32, (256, 256), 0).astype(F32).astype(BF16)

    def products(group):
        hi = jnp.broadcast_to(key_hi[pl.ds(group, 1), :].astype(BF16), (256, 256))
        lo = jnp.broadcast_to(key_lo[pl.ds(group, 1), :].astype(BF16), (256, 256))
        left = jnp.where(hi == rows, BF16(1), BF16(0)).astype(PRODUCT)
        right = jnp.where(lo == rows, BF16(1), BF16(0)).astype(PRODUCT)
        return dot(left, right, NT).reshape(16, 16, 256)

    def one_pair(pair, carry):
        both = jnp.concatenate([products(2 * pair), products(2 * pair + 1)], axis=1)
        at = pl.ds(pl.multiple_of(pair * 32, 32), 32)
        table[:, at, :] = both.astype(COUNT)
        return carry

    copies = []
    for chunk in range(CHUNKS):
        lax.fori_loop(
            chunk * CHUNK // 32, (chunk + 1) * CHUNK // 32, one_pair, 0, unroll=UNROLL
        )
        at = pl.ds(chunk * CHUNK, CHUNK)
        copies.append(start(table.at[:, at], table_hbm.at[:, at], table_sems.at[chunk]))
    for half in range(2):
        for block in range(2 * half, 2 * half + 2):
            at = slice(block * 512, (block + 1) * 512)
            total = jnp.zeros((512, WIDTH), F32)
            for hi in range(LOCAL):
                total = total + dot(
                    table[hi, at, :].astype(BF16), features[hi * 256 : (hi + 1) * 256, :]
                )
            summed[at, :] = total
        at = pl.ds(half * 1024, 1024)
        copies.append(start(summed.at[at], summed_hbm.at[at], summed_sems.at[half]))
    for copy in copies:
        copy.wait()


def count(neighbours, counts, features):
    return pl.pallas_call(
        count_kernel,
        out_shape=(
            pltpu.HBM((LOCAL + REMOTE, NODES, WIDTH), COUNT),
            pltpu.HBM((NODES, WIDTH), F32),
        ),
        in_specs=[HBM] * 3,
        out_specs=[HBM] * 2,
        scratch_shapes=[
            pltpu.VMEM((FAN, NODES), I32),
            pltpu.VMEM((1, NODES), I32),
            pltpu.VMEM((NODES, WIDTH), BF16),
            pltpu.VMEM((LOCAL + REMOTE, NODES, WIDTH), COUNT),
            pltpu.VMEM((NODES, WIDTH), F32),
            pltpu.VMEM((GROUPS, 256), F32),
            pltpu.VMEM((GROUPS, 256), F32),
            DMA((3,)),
            DMA((CHUNKS,)),
            DMA((CHUNKS,)),
        ],
        compiler_params=pltpu.CompilerParams(vmem_limit_bytes=40 << 20),
        cost_estimate=pl.CostEstimate(
            flops=2 * NODES * 4096 * WIDTH * 2, bytes_accessed=20 << 20, transcendentals=0
        ),
        name="count",
    )(*in_hbm(neighbours, counts, features))


def node_kernel(
    arrived,
    table_hbm,
    summed_hbm,
    features_hbm,
    counts_hbm,
    cotangent_hbm,
    self_weight_hbm,
    neighbour_weight_hbm,
    activations_hbm,
    grad_pre_hbm,
    edge_hbm,
    message_hbm,
    table,
    summed,
    features,
    counts,
    cotangent,
    self_weight,
    neighbour_weight,
    activations,
    grad_pre,
    edge,
    mean,
    message,
    weights,
    parts,
    small_sems,
    in_sems,
    out_sems,
    message_sems,
):
    get_small = [
        start(counts_hbm, counts, small_sems.at[0]),
        start(self_weight_hbm, self_weight, small_sems.at[1]),
        start(neighbour_weight_hbm, neighbour_weight, small_sems.at[2]),
    ]
    get = []
    for step in range(STEPS):
        at = pl.ds(CUTS[step], CUTS[step + 1] - CUTS[step])
        late = min(step, 1)
        get.append(
            [
                start(
                    table_hbm.at[pl.ds(LOCAL, REMOTE), at],
                    table.at[:, at],
                    in_sems.at[1, step],
                    late,
                ),
                start(summed_hbm.at[at], summed.at[at], in_sems.at[2, step], late),
                start(features_hbm.at[at], features.at[at], in_sems.at[0, step], late),
                start(cotangent_hbm.at[at], cotangent.at[at], in_sems.at[3, step], late),
            ]
        )
    for copy in get_small:
        copy.wait()
    inverse = (1.0 / counts[...].astype(F32)).T
    remote = arrived[...].reshape(NODES, WIDTH)
    scales = [
        jnp.concatenate(
            [
                jnp.broadcast_to(inverse[:, part : part + 1], (128, 256))
                for part in range(CUTS[step] // 128, CUTS[step + 1] // 128)
            ],
            axis=0,
        )
        for step in range(STEPS)
    ]

    def gather(step):
        for copy in get[step]:
            copy.wait()
        at = slice(CUTS[step], CUTS[step + 1])
        total = summed[at, :]
        for hi in range(REMOTE):
            total = total + dot(table[hi, at, :].astype(BF16), remote[hi * 256 : (hi + 1) * 256])
        return (total * scales[step]).astype(BF16)

    def update(step, block_mean):
        at = slice(CUTS[step], CUTS[step + 1])
        mean[at, :] = block_mean
        pre = dot(features[at, :], self_weight[...]) + dot(block_mean, neighbour_weight[...])
        sigmoid = 0.5 * jnp.tanh(0.5 * pre) + 0.5
        activations[at, :] = (pre * sigmoid).astype(BF16)
        slope = sigmoid * (1.0 + pre * (1.0 - sigmoid))
        block_grad = (cotangent[at, :].astype(F32) * slope).astype(BF16)
        grad_pre[at, :] = block_grad
        edge[at, :] = (dot(block_grad, neighbour_weight[...], NT) * scales[step]).astype(BF16)
        for part, left in ((0, features[at, :]), (1, block_mean)):
            product = dot(left, block_grad, TN)
            for half in range(2):
                where = (half, slice(part * WIDTH, (part + 1) * WIDTH))
                piece = product[:, half * 128 : (half + 1) * 128]
                weights[where] = piece if step == 0 else weights[where] + piece

    now = gather(0)
    for step in range(STEPS):
        later = gather(step + 1) if step + 1 < STEPS else None
        update(step, now)
        now = later
    put = []
    for half in range(2):
        for row in range(4):
            parts[pl.ds(half * 4 + row, PEERS, stride=8), :] = weights[
                half, pl.ds(row, PEERS, stride=4), :
            ]
    message[:, 32:40, :] = parts[...].reshape(PEERS, 8, 128).astype(BF16)
    put = [
        start(activations, activations_hbm, out_sems.at[0], 1),
        start(grad_pre, grad_pre_hbm, out_sems.at[1], 1),
        start(edge, edge_hbm, out_sems.at[2], 1),
    ]
    for hi in range(REMOTE):
        added = dot(table[hi].astype(BF16), edge[...], TN).astype(BF16).reshape(16, 16, WIDTH)
        message[hi * 16 : (hi + 1) * 16, 0:16, :] = added[:, :, :128]
        message[hi * 16 : (hi + 1) * 16, 16:32, :] = added[:, :, 128:]
        if (hi + 1) % PIECE == 0:
            peers = pl.ds((hi + 1 - PIECE) * 16, PIECE * 16)
            put.append(start(message.at[peers], message_hbm.at[peers], message_sems.at[hi]))
    for copy in put:
        copy.wait()


def node(
    arrived, table, summed, features, counts, cotangent, self_weight, neighbour_weight
):
    rows = pltpu.VMEM((NODES, WIDTH), BF16)
    return pl.pallas_call(
        node_kernel,
        out_shape=(
            pltpu.HBM((NODES, WIDTH), BF16),
            pltpu.HBM((NODES, WIDTH), BF16),
            pltpu.HBM((NODES, WIDTH), BF16),
            pltpu.HBM((PEERS, MESSAGE, 128), BF16),
        ),
        in_specs=[VMEM] + [HBM] * 7,
        out_specs=[HBM] * 4,
        scratch_shapes=[
            pltpu.VMEM((REMOTE, NODES, WIDTH), COUNT),
            pltpu.VMEM((NODES, WIDTH), F32),
            rows,
            pltpu.VMEM((16, 128), I32),
            rows,
            pltpu.VMEM((WIDTH, WIDTH), BF16),
            pltpu.VMEM((WIDTH, WIDTH), BF16),
            rows,
            rows,
            rows,
            rows,
            pltpu.VMEM((PEERS, MESSAGE, 128), BF16),
            pltpu.VMEM((2, 2 * WIDTH, 128), F32),
            pltpu.VMEM((8 * PEERS, 128), F32),
            DMA((3,)),
            DMA((4, STEPS)),
            DMA((3,)),
            DMA((REMOTE,)),
        ],
        compiler_params=pltpu.CompilerParams(vmem_limit_bytes=40 << 20),
        cost_estimate=pl.CostEstimate(
            flops=2 * NODES * 2048 * WIDTH * 2, bytes_accessed=16 << 20, transcendentals=0
        ),
        name="node",
    )(
        arrived,
        *in_hbm(table, summed, features, counts, cotangent, self_weight, neighbour_weight),
    )


def local_kernel(
    table_hbm,
    edge_hbm,
    grad_pre_hbm,
    self_weight_hbm,
    lists_hbm,
    grads_hbm,
    ids,
    table,
    edge,
    grad_pre,
    self_weight,
    lists,
    grads,
    in_sems,
    table_sems,
    out_sems,
):
    get_edge = start(edge_hbm, edge, in_sems.at[0])
    get = [start(table_hbm.at[hi], table.at[hi], table_sems.at[hi]) for hi in range(LOCAL)]
    get_small = [
        start(grad_pre_hbm, grad_pre, in_sems.at[1]),
        start(self_weight_hbm, self_weight, in_sems.at[2]),
        start(lists_hbm, lists, in_sems.at[3]),
    ]
    for copy in get_small:
        copy.wait()
    ids[...] = flatten_lanes((lists[...] >> 8).astype(F32)) * 256.0 + flatten_lanes(
        (lists[...] & 255).astype(F32)
    )
    get_edge.wait()
    for copy in get:
        copy.wait()
    for hi in range(LOCAL):
        at = slice(hi * 256, (hi + 1) * 256)
        grads[at, :] = dot(table[hi].astype(BF16), edge[...], TN) + dot(grad_pre[at, :], self_weight[...], NT)
    start(grads, grads_hbm, out_sems.at[0]).wait()


def local(table, edge, grad_pre, self_weight, lists):
    rows = pltpu.VMEM((NODES, WIDTH), BF16)
    return pl.pallas_call(
        local_kernel,
        out_shape=(
            pltpu.HBM((NODES, WIDTH), F32),
            pltpu.HBM((4, 256), F32),
        ),
        in_specs=[HBM] * 5,
        out_specs=[HBM, VMEM],
        scratch_shapes=[
            pltpu.VMEM((LOCAL, NODES, WIDTH), COUNT),
            rows,
            rows,
            pltpu.VMEM((WIDTH, WIDTH), BF16),
            pltpu.VMEM((8, PEERS), I32),
            pltpu.VMEM((NODES, WIDTH), F32),
            DMA((4,)),
            DMA((LOCAL,)),
            DMA((1,)),
        ],
        compiler_params=pltpu.CompilerParams(vmem_limit_bytes=40 << 20),
        cost_estimate=pl.CostEstimate(
            flops=2 * NODES * 2048 * WIDTH, bytes_accessed=14 << 20, transcendentals=0
        ),
        name="local",
    )(*in_hbm(table, edge, grad_pre, self_weight, lists))


def finish_kernel(
    returned,
    grads_hbm,
    ids_hbm,
    hub_hbm,
    grad_features_hbm,
    grad_weights,
    grads,
    ids,
    hub,
    totals,
    sems,
    put_sems,
):
    get_ids = start(ids_hbm, ids, sems.at[0])
    get_hub = start(hub_hbm, hub, sems.at[1])
    get_grads = start(grads_hbm, grads, sems.at[2])
    sides = [returned[:, 0:16, :].astype(F32), returned[:, 16:32, :].astype(F32)]
    bound = jnp.concatenate([side[:, :8].reshape(8 * PEERS, 128) for side in sides], axis=1)
    bound = bound.astype(BF16)
    hubs = jnp.concatenate([jnp.sum(side[:, 8:], axis=0) for side in sides], axis=1)
    high = hubs.astype(BF16).astype(F32)
    hubs = jnp.concatenate([high, hubs - high], axis=0).astype(BF16)
    weights = jnp.sum(returned[:, 32:40, :].astype(F32), axis=0)
    grad_weights[...] = jnp.concatenate([weights[:4], weights[4:]], axis=1)
    get_ids.wait()
    get_hub.wait()
    get_grads.wait()
    put = []
    rows = lax.broadcasted_iota(I32, (BLOCK, 256), 0).astype(F32).astype(BF16)
    twice = jnp.concatenate([hub[...], hub[...]], axis=1)
    for block in range(BLOCKS):
        at = slice(block * BLOCK, (block + 1) * BLOCK)
        offset = ids[...] - block * 256.0
        inside = (offset >= 0.0) & (offset < 256.0)
        keys = jnp.where(inside, offset, -1.0).astype(BF16)
        hot = jnp.concatenate(
            [
                jnp.where(
                    jnp.broadcast_to(keys[part : part + 1, :], (BLOCK, 256)) == rows,
                    BF16(1),
                    BF16(0),
                )
                for part in range(4)
            ],
            axis=1,
        )
        hub_hot = one_hot(
            jnp.broadcast_to(twice - block * BLOCK, (BLOCK, 16)), (BLOCK, 16), 0
        )
        totals[at, :] = grads[at, :] + dot(hot, bound) + dot(hub_hot, hubs)
        if (block + 1) % FINISH_PIECE == 0:
            piece = pl.ds((block + 1 - FINISH_PIECE) * BLOCK, FINISH_PIECE * BLOCK)
            put.append(start(totals.at[piece], grad_features_hbm.at[piece], put_sems.at[block]))
    for copy in put:
        copy.wait()


def finish(returned, grads, ids, hub):
    return pl.pallas_call(
        finish_kernel,
        out_shape=(
            pltpu.HBM((NODES, WIDTH), F32),
            jax.ShapeDtypeStruct((4, WIDTH), F32),
        ),
        in_specs=[VMEM, HBM, HBM, HBM],
        out_specs=[HBM, VMEM],
        scratch_shapes=[
            pltpu.VMEM((NODES, WIDTH), F32),
            pltpu.VMEM((4, 256), F32),
            pltpu.VMEM((1, 8), I32),
            pltpu.VMEM((NODES, WIDTH), F32),
            DMA((3,)),
            DMA((BLOCKS,)),
        ],
        compiler_params=pltpu.CompilerParams(vmem_limit_bytes=32 << 20),
        cost_estimate=pl.CostEstimate(
            flops=2 * NODES * 1024 * WIDTH, bytes_accessed=6 << 20, transcendentals=0
        ),
        name="finish",
    )(returned, *in_hbm(grads, ids, hub))


def body(
    features, self_weight, neighbour_weight, send_lists, hub_nodes, neighbours, counts, cotangent
):
    lists = send_lists[0].T
    packed = pack(features, lists, hub_nodes)
    arrived = lax.all_to_all(packed, "dom", split_axis=0, concat_axis=0, tiled=True)
    table, summed = count(neighbours.T, counts.reshape(1, NODES), features)
    activations, grad_pre, edge, message = node(
        arrived,
        table,
        summed,
        features,
        counts.reshape(16, 128),
        cotangent,
        self_weight,
        neighbour_weight,
    )
    returned = lax.all_to_all(message, "dom", split_axis=0, concat_axis=0, tiled=True)
    grads, ids = local(table, edge, grad_pre, self_weight, lists)
    grad_features, grad_weights = finish(returned, grads, ids, hub_nodes)
    return (activations, grad_features, grad_weights)


def solution(mesh):
    in_specs = (
        P("dom", None),
        P(),
        P(),
        P("dom", None, None),
        P("dom", None),
        P("dom", None),
        P("dom"),
        P("dom", None),
    )
    out_specs = (P("dom", None), P("dom", None), P("dom", None))
    return jax.shard_map(body, mesh=mesh, in_specs=in_specs, out_specs=out_specs, check_vma=False)
```

```python
import jax
import jax.numpy as jnp
from jax import lax
from jax.experimental import pallas as pl
from jax.experimental.pallas import tpu as pltpu
from jax.sharding import PartitionSpec as P

BF16 = jnp.bfloat16
COUNT = jnp.float8_e4m3fn
PRODUCT = jnp.float8_e4m3fn
UNROLL = 16
F32 = jnp.float32
I32 = jnp.int32
NODES = 2048
WIDTH = 256
PEERS = 128
SLOTS = 16
FAN = 16
GROUPS = NODES // 16
LOCAL = 8
REMOTE = 8
VMEM = pl.BlockSpec(memory_space=pltpu.VMEM)
HBM = pl.BlockSpec(memory_space=pltpu.HBM)
DMA = pltpu.SemaphoreType.DMA
BLOCK = 256
BLOCKS = NODES // BLOCK
MESSAGE = 40
CUTS = (0, 256, 768, 1280, 2048)
STEPS = len(CUTS) - 1
PIECES = {3: (0, 4), 6: (4, 7), 7: (7, 8)}
FINISH_PIECE = 2
NN = (((1,), (0,)), ((), ()))
NT = (((1,), (1,)), ((), ()))
TN = (((0,), (0,)), ((), ()))


def dot(a, b, dims=NN):
    return lax.dot_general(a, b, dims, preferred_element_type=F32)


def one_hot(keys, shape, axis):
    return jnp.where(keys == lax.broadcasted_iota(I32, shape, axis), F32(1), F32(0)).astype(BF16)


def in_hbm(*arrays):
    return [pltpu.with_memory_space_constraint(array, pltpu.HBM) for array in arrays]


def start(source, target, semaphore, priority=0):
    copy = pltpu.make_async_copy(source, target, semaphore)
    copy.start(priority=priority)
    return copy


def rows_of(block):
    return pl.ds(block * BLOCK, BLOCK)


def flatten_lanes(values):
    k, n = values.shape
    per = 256 // k
    lane = lax.broadcasted_iota(I32, (k, 256), 1)
    own = lax.broadcasted_iota(I32, (k, 256), 0) == (lane & (k - 1))
    tiled = dot(values.astype(BF16), jnp.where(own, F32(1), F32(0)).astype(BF16), TN)
    shape = (n // per, per, 256)
    shift = k.bit_length() - 1
    mine = (lax.broadcasted_iota(I32, shape, 2) >> shift) == lax.broadcasted_iota(I32, shape, 1)
    return jnp.sum(jnp.where(mine, tiled.reshape(shape), F32(0)), axis=1)


def pack_kernel(features_hbm, lists_hbm, hub_hbm, packed, features, lists, hub, sems):
    get_lists = start(lists_hbm, lists, sems.at[0])
    get_hub = start(hub_hbm, hub, sems.at[1])
    get_features = start(features_hbm, features, sems.at[2])
    get_lists.wait()
    get_hub.wait()
    get_features.wait()
    ids = flatten_lanes((lists[...] >> 8).astype(F32)) * 256.0 + flatten_lanes(
        (lists[...] & 255).astype(F32)
    )
    hub_ids = jnp.concatenate([hub[...].astype(F32), jnp.full((1, 120), -1.0, F32)], axis=1)
    ids = jnp.concatenate([ids[part : part + 1] for part in range(4)] + [hub_ids], axis=1)
    rows = lax.broadcasted_iota(I32, (256, 1152), 0).astype(F32).astype(BF16)
    picked = jnp.zeros((1152, WIDTH), F32)
    for chunk in range(8):
        offset = ids - chunk * 256.0
        inside = (offset >= 0.0) & (offset < 256.0)
        keys = jnp.where(inside, offset, -1.0).astype(BF16)
        hot = jnp.where(jnp.broadcast_to(keys, (256, 1152)) == rows, BF16(1), BF16(0))
        picked = picked + dot(hot, features[chunk * 256 : (chunk + 1) * 256, :], TN)
    hubs = jnp.broadcast_to(picked[8 * PEERS : 8 * PEERS + 8][None], (PEERS, 8, WIDTH))
    bound = picked[: 8 * PEERS].reshape(PEERS, 8, WIDTH)
    packed[...] = jnp.concatenate([bound, hubs], axis=1).astype(BF16)


def pack(features, lists, hub):
    return pl.pallas_call(
        pack_kernel,
        out_shape=pltpu.HBM((PEERS, SLOTS, WIDTH), BF16),
        in_specs=[HBM] * 3,
        out_specs=VMEM,
        scratch_shapes=[
            pltpu.VMEM((NODES, WIDTH), BF16),
            pltpu.VMEM((8, PEERS), I32),
            pltpu.VMEM((1, 8), I32),
            DMA((3,)),
        ],
        compiler_params=pltpu.CompilerParams(vmem_limit_bytes=24 << 20),
        cost_estimate=pl.CostEstimate(
            flops=2 * 1040 * NODES * WIDTH, bytes_accessed=2 << 20, transcendentals=0
        ),
        name="pack",
    )(*in_hbm(features, lists, hub))


CHUNK = 512
CHUNKS = NODES // CHUNK


def count_kernel(
    neighbours_hbm,
    counts_hbm,
    features_hbm,
    table_hbm,
    summed_hbm,
    neighbours,
    counts,
    features,
    table,
    summed,
    key_hi,
    key_lo,
    in_sems,
    table_sems,
    summed_sems,
):
    get_neighbours = start(neighbours_hbm, neighbours, in_sems.at[0])
    get_counts = start(counts_hbm, counts, in_sems.at[1])
    get_features = start(features_hbm, features, in_sems.at[2])
    get_neighbours.wait()
    index = neighbours[...]
    bound = index - NODES
    hub = bound - 8 * PEERS
    index = jnp.where(
        index < NODES,
        index,
        jnp.where(
            hub < 0,
            NODES + ((bound >> 3) << 4) + (bound & 7),
            NODES + ((hub >> 3) << 4) + 8 + (hub & 7),
        ),
    )
    get_counts.wait()
    usable = lax.broadcasted_iota(I32, index.shape, 0) < counts[...]
    index = jnp.where(usable, index, 4096)
    lane = lax.broadcasted_iota(I32, (GROUPS, 256), 1)
    key_hi[...] = flatten_lanes((index >> 8).astype(F32)) * 16.0 + (lane >> 4).astype(F32)
    key_lo[...] = flatten_lanes((index & 255).astype(F32))
    get_features.wait()

    rows = lax.broadcasted_iota(I32, (256, 256), 0).astype(F32).astype(BF16)

    def products(group):
        hi = jnp.broadcast_to(key_hi[pl.ds(group, 1), :].astype(BF16), (256, 256))
        lo = jnp.broadcast_to(key_lo[pl.ds(group, 1), :].astype(BF16), (256, 256))
        left = jnp.where(hi == rows, BF16(1), BF16(0)).astype(PRODUCT)
        right = jnp.where(lo == rows, BF16(1), BF16(0)).astype(PRODUCT)
        return dot(left, right, NT).reshape(16, 16, 256)

    def one_pair(pair, carry):
        both = jnp.concatenate([products(2 * pair), products(2 * pair + 1)], axis=1)
        at = pl.ds(pl.multiple_of(pair * 32, 32), 32)
        table[:, at, :] = both.astype(COUNT)
        return carry

    copies = []
    for chunk in range(CHUNKS):
        lax.fori_loop(
            chunk * CHUNK // 32, (chunk + 1) * CHUNK // 32, one_pair, 0, unroll=UNROLL
        )
        at = pl.ds(chunk * CHUNK, CHUNK)
        copies.append(start(table.at[:, at], table_hbm.at[:, at], table_sems.at[chunk]))
    for half in range(2):
        for block in range(2 * half, 2 * half + 2):
            at = slice(block * 512, (block + 1) * 512)
            total = jnp.zeros((512, WIDTH), F32)
            for hi in range(LOCAL):
                total = total + dot(
                    table[hi, at, :].astype(BF16), features[hi * 256 : (hi + 1) * 256, :]
                )
            summed[at, :] = total
        at = pl.ds(half * 1024, 1024)
        copies.append(start(summed.at[at], summed_hbm.at[at], summed_sems.at[half]))
    for copy in copies:
        copy.wait()


def count(neighbours, counts, features):
    return pl.pallas_call(
        count_kernel,
        out_shape=(
            pltpu.HBM((LOCAL + REMOTE, NODES, WIDTH), COUNT),
            pltpu.HBM((NODES, WIDTH), F32),
        ),
        in_specs=[HBM] * 3,
        out_specs=[HBM] * 2,
        scratch_shapes=[
            pltpu.VMEM((FAN, NODES), I32),
            pltpu.VMEM((1, NODES), I32),
            pltpu.VMEM((NODES, WIDTH), BF16),
            pltpu.VMEM((LOCAL + REMOTE, NODES, WIDTH), COUNT),
            pltpu.VMEM((NODES, WIDTH), F32),
            pltpu.VMEM((GROUPS, 256), F32),
            pltpu.VMEM((GROUPS, 256), F32),
            DMA((3,)),
            DMA((CHUNKS,)),
            DMA((CHUNKS,)),
        ],
        compiler_params=pltpu.CompilerParams(vmem_limit_bytes=40 << 20),
        cost_estimate=pl.CostEstimate(
            flops=2 * NODES * 4096 * WIDTH * 2, bytes_accessed=20 << 20, transcendentals=0
        ),
        name="count",
    )(*in_hbm(neighbours, counts, features))


def node_kernel(
    arrived_hbm,
    table_hbm,
    summed_hbm,
    features_hbm,
    counts_hbm,
    cotangent_hbm,
    self_weight_hbm,
    neighbour_weight_hbm,
    activations_hbm,
    grad_pre_hbm,
    edge_hbm,
    message_hbm,
    arrived,
    table,
    summed,
    features,
    counts,
    cotangent,
    self_weight,
    neighbour_weight,
    activations,
    grad_pre,
    edge,
    mean,
    message,
    weights,
    parts,
    small_sems,
    in_sems,
    out_sems,
    message_sems,
):
    get_small = [
        start(arrived_hbm, arrived, small_sems.at[3]),
        start(counts_hbm, counts, small_sems.at[0]),
        start(self_weight_hbm, self_weight, small_sems.at[1]),
        start(neighbour_weight_hbm, neighbour_weight, small_sems.at[2]),
    ]
    get = []
    for step in range(STEPS):
        at = pl.ds(CUTS[step], CUTS[step + 1] - CUTS[step])
        late = min(step, 1)
        get.append(
            [
                start(
                    table_hbm.at[pl.ds(LOCAL, REMOTE), at],
                    table.at[:, at],
                    in_sems.at[1, step],
                    late,
                ),
                start(summed_hbm.at[at], summed.at[at], in_sems.at[2, step], late),
                start(features_hbm.at[at], features.at[at], in_sems.at[0, step], late),
                start(cotangent_hbm.at[at], cotangent.at[at], in_sems.at[3, step], late),
            ]
        )
    for copy in get_small:
        copy.wait()
    inverse = (1.0 / counts[...].astype(F32)).T
    remote = arrived[...].reshape(NODES, WIDTH)
    scales = [
        jnp.concatenate(
            [
                jnp.broadcast_to(inverse[:, part : part + 1], (128, 256))
                for part in range(CUTS[step] // 128, CUTS[step + 1] // 128)
            ],
            axis=0,
        )
        for step in range(STEPS)
    ]

    def gather(step):
        for copy in get[step]:
            copy.wait()
        at = slice(CUTS[step], CUTS[step + 1])
        total = summed[at, :]
        for hi in range(REMOTE):
            total = total + dot(table[hi, at, :].astype(BF16), remote[hi * 256 : (hi + 1) * 256])
        return (total * scales[step]).astype(BF16)

    def update(step, block_mean):
        at = slice(CUTS[step], CUTS[step + 1])
        mean[at, :] = block_mean
        pre = dot(features[at, :], self_weight[...]) + dot(block_mean, neighbour_weight[...])
        sigmoid = 0.5 * jnp.tanh(0.5 * pre) + 0.5
        activations[at, :] = (pre * sigmoid).astype(BF16)
        slope = sigmoid * (1.0 + pre * (1.0 - sigmoid))
        block_grad = (cotangent[at, :].astype(F32) * slope).astype(BF16)
        grad_pre[at, :] = block_grad
        edge[at, :] = (dot(block_grad, neighbour_weight[...], NT) * scales[step]).astype(BF16)
        for part, left in ((0, features[at, :]), (1, block_mean)):
            product = dot(left, block_grad, TN)
            for half in range(2):
                where = (half, slice(part * WIDTH, (part + 1) * WIDTH))
                piece = product[:, half * 128 : (half + 1) * 128]
                weights[where] = piece if step == 0 else weights[where] + piece

    now = gather(0)
    for step in range(STEPS):
        later = gather(step + 1) if step + 1 < STEPS else None
        update(step, now)
        now = later
    put = []
    for half in range(2):
        for row in range(4):
            parts[pl.ds(half * 4 + row, PEERS, stride=8), :] = weights[
                half, pl.ds(row, PEERS, stride=4), :
            ]
    message[:, 32:40, :] = parts[...].reshape(PEERS, 8, 128).astype(BF16)
    put = [
        start(activations, activations_hbm, out_sems.at[0], 1),
        start(grad_pre, grad_pre_hbm, out_sems.at[1], 1),
        start(edge, edge_hbm, out_sems.at[2], 1),
    ]
    for hi in range(REMOTE):
        added = dot(table[hi].astype(BF16), edge[...], TN).astype(BF16).reshape(16, 16, WIDTH)
        message[hi * 16 : (hi + 1) * 16, 0:16, :] = added[:, :, :128]
        message[hi * 16 : (hi + 1) * 16, 16:32, :] = added[:, :, 128:]
        if hi in PIECES:
            first, last = PIECES[hi]
            peers = pl.ds(first * 16, (last - first) * 16)
            put.append(start(message.at[peers], message_hbm.at[peers], message_sems.at[hi]))
    for copy in put:
        copy.wait()


def node(
    arrived, table, summed, features, counts, cotangent, self_weight, neighbour_weight
):
    rows = pltpu.VMEM((NODES, WIDTH), BF16)
    return pl.pallas_call(
        node_kernel,
        out_shape=(
            pltpu.HBM((NODES, WIDTH), BF16),
            pltpu.HBM((NODES, WIDTH), BF16),
            pltpu.HBM((NODES, WIDTH), BF16),
            pltpu.HBM((PEERS, MESSAGE, 128), BF16),
        ),
        in_specs=[HBM] * 8,
        out_specs=[HBM] * 4,
        scratch_shapes=[
            pltpu.VMEM((PEERS, SLOTS, WIDTH), BF16),
            pltpu.VMEM((REMOTE, NODES, WIDTH), COUNT),
            pltpu.VMEM((NODES, WIDTH), F32),
            rows,
            pltpu.VMEM((16, 128), I32),
            rows,
            pltpu.VMEM((WIDTH, WIDTH), BF16),
            pltpu.VMEM((WIDTH, WIDTH), BF16),
            rows,
            rows,
            rows,
            rows,
            pltpu.VMEM((PEERS, MESSAGE, 128), BF16),
            pltpu.VMEM((2, 2 * WIDTH, 128), F32),
            pltpu.VMEM((8 * PEERS, 128), F32),
            DMA((4,)),
            DMA((4, STEPS)),
            DMA((3,)),
            DMA((REMOTE,)),
        ],
        compiler_params=pltpu.CompilerParams(vmem_limit_bytes=40 << 20),
        cost_estimate=pl.CostEstimate(
            flops=2 * NODES * 2048 * WIDTH * 2, bytes_accessed=16 << 20, transcendentals=0
        ),
        name="node",
    )(
        *in_hbm(
            arrived,
            table,
            summed,
            features,
            counts,
            cotangent,
            self_weight,
            neighbour_weight,
        )
    )


def local_kernel(
    table_hbm,
    edge_hbm,
    grad_pre_hbm,
    self_weight_hbm,
    lists_hbm,
    grads_hbm,
    ids,
    table,
    edge,
    grad_pre,
    self_weight,
    lists,
    grads,
    in_sems,
    table_sems,
    out_sems,
):
    get_edge = start(edge_hbm, edge, in_sems.at[0])
    get = [start(table_hbm.at[hi], table.at[hi], table_sems.at[hi]) for hi in range(LOCAL)]
    get_small = [
        start(grad_pre_hbm, grad_pre, in_sems.at[1]),
        start(self_weight_hbm, self_weight, in_sems.at[2]),
        start(lists_hbm, lists, in_sems.at[3]),
    ]
    for copy in get_small:
        copy.wait()
    ids[...] = flatten_lanes((lists[...] >> 8).astype(F32)) * 256.0 + flatten_lanes(
        (lists[...] & 255).astype(F32)
    )
    get_edge.wait()
    for copy in get:
        copy.wait()
    for hi in range(LOCAL):
        at = slice(hi * 256, (hi + 1) * 256)
        grads[at, :] = dot(table[hi].astype(BF16), edge[...], TN) + dot(grad_pre[at, :], self_weight[...], NT)
    start(grads, grads_hbm, out_sems.at[0]).wait()


def local(table, edge, grad_pre, self_weight, lists):
    rows = pltpu.VMEM((NODES, WIDTH), BF16)
    return pl.pallas_call(
        local_kernel,
        out_shape=(
            pltpu.HBM((NODES, WIDTH), F32),
            pltpu.HBM((4, 256), F32),
        ),
        in_specs=[HBM] * 5,
        out_specs=[HBM, VMEM],
        scratch_shapes=[
            pltpu.VMEM((LOCAL, NODES, WIDTH), COUNT),
            rows,
            rows,
            pltpu.VMEM((WIDTH, WIDTH), BF16),
            pltpu.VMEM((8, PEERS), I32),
            pltpu.VMEM((NODES, WIDTH), F32),
            DMA((4,)),
            DMA((LOCAL,)),
            DMA((1,)),
        ],
        compiler_params=pltpu.CompilerParams(vmem_limit_bytes=40 << 20),
        cost_estimate=pl.CostEstimate(
            flops=2 * NODES * 2048 * WIDTH, bytes_accessed=14 << 20, transcendentals=0
        ),
        name="local",
    )(*in_hbm(table, edge, grad_pre, self_weight, lists))


def finish_kernel(
    returned,
    grads_hbm,
    ids_hbm,
    hub_hbm,
    grad_features_hbm,
    grad_weights,
    grads,
    ids,
    hub,
    totals,
    sems,
    put_sems,
):
    get_ids = start(ids_hbm, ids, sems.at[0])
    get_hub = start(hub_hbm, hub, sems.at[1])
    get_grads = start(grads_hbm, grads, sems.at[2])
    sides = [returned[:, 0:16, :].astype(F32), returned[:, 16:32, :].astype(F32)]
    bound = jnp.concatenate([side[:, :8].reshape(8 * PEERS, 128) for side in sides], axis=1)
    bound = bound.astype(BF16)
    hubs = jnp.concatenate([jnp.sum(side[:, 8:], axis=0) for side in sides], axis=1)
    high = hubs.astype(BF16).astype(F32)
    hubs = jnp.concatenate([high, hubs - high], axis=0).astype(BF16)
    weights = jnp.sum(returned[:, 32:40, :].astype(F32), axis=0)
    grad_weights[...] = jnp.concatenate([weights[:4], weights[4:]], axis=1)
    get_ids.wait()
    get_hub.wait()
    get_grads.wait()
    put = []
    rows = lax.broadcasted_iota(I32, (BLOCK, 256), 0).astype(F32).astype(BF16)
    twice = jnp.concatenate([hub[...], hub[...]], axis=1)
    for block in range(BLOCKS):
        at = slice(block * BLOCK, (block + 1) * BLOCK)
        offset = ids[...] - block * 256.0
        inside = (offset >= 0.0) & (offset < 256.0)
        keys = jnp.where(inside, offset, -1.0).astype(BF16)
        hot = jnp.concatenate(
            [
                jnp.where(
                    jnp.broadcast_to(keys[part : part + 1, :], (BLOCK, 256)) == rows,
                    BF16(1),
                    BF16(0),
                )
                for part in range(4)
            ],
            axis=1,
        )
        hub_hot = one_hot(
            jnp.broadcast_to(twice - block * BLOCK, (BLOCK, 16)), (BLOCK, 16), 0
        )
        totals[at, :] = grads[at, :] + dot(hot, bound) + dot(hub_hot, hubs)
        if (block + 1) % FINISH_PIECE == 0:
            piece = pl.ds((block + 1 - FINISH_PIECE) * BLOCK, FINISH_PIECE * BLOCK)
            put.append(start(totals.at[piece], grad_features_hbm.at[piece], put_sems.at[block]))
    for copy in put:
        copy.wait()


def finish(returned, grads, ids, hub):
    return pl.pallas_call(
        finish_kernel,
        out_shape=(
            pltpu.HBM((NODES, WIDTH), F32),
            jax.ShapeDtypeStruct((4, WIDTH), F32),
        ),
        in_specs=[VMEM, HBM, HBM, HBM],
        out_specs=[HBM, VMEM],
        scratch_shapes=[
            pltpu.VMEM((NODES, WIDTH), F32),
            pltpu.VMEM((4, 256), F32),
            pltpu.VMEM((1, 8), I32),
            pltpu.VMEM((NODES, WIDTH), F32),
            DMA((3,)),
            DMA((BLOCKS,)),
        ],
        compiler_params=pltpu.CompilerParams(vmem_limit_bytes=32 << 20),
        cost_estimate=pl.CostEstimate(
            flops=2 * NODES * 1024 * WIDTH, bytes_accessed=6 << 20, transcendentals=0
        ),
        name="finish",
    )(returned, *in_hbm(grads, ids, hub))


def body(
    features, self_weight, neighbour_weight, send_lists, hub_nodes, neighbours, counts, cotangent
):
    lists = send_lists[0].T
    packed = pack(features, lists, hub_nodes)
    arrived = lax.all_to_all(packed, "dom", split_axis=0, concat_axis=0, tiled=True)
    table, summed = count(neighbours.T, counts.reshape(1, NODES), features)
    activations, grad_pre, edge, message = node(
        arrived,
        table,
        summed,
        features,
        counts.reshape(16, 128),
        cotangent,
        self_weight,
        neighbour_weight,
    )
    returned = lax.all_to_all(message, "dom", split_axis=0, concat_axis=0, tiled=True)
    grads, ids = local(table, edge, grad_pre, self_weight, lists)
    grad_features, grad_weights = finish(returned, grads, ids, hub_nodes)
    return (activations, grad_features, grad_weights)


def solution(mesh):
    in_specs = (
        P("dom", None),
        P(),
        P(),
        P("dom", None, None),
        P("dom", None),
        P("dom", None),
        P("dom"),
        P("dom", None),
    )
    out_specs = (P("dom", None), P("dom", None), P("dom", None))
    return jax.shard_map(body, mesh=mesh, in_specs=in_specs, out_specs=out_specs, check_vma=False)
```

```python
import jax
import jax.numpy as jnp
from jax import lax
from jax.experimental import pallas as pl
from jax.experimental.pallas import tpu as pltpu
from jax.sharding import PartitionSpec as P

BF16 = jnp.bfloat16
COUNT = jnp.float8_e4m3fn
PRODUCT = jnp.float8_e4m3fn
UNROLL = 16
F32 = jnp.float32
I32 = jnp.int32
NODES = 2048
WIDTH = 256
PEERS = 128
SLOTS = 16
FAN = 16
GROUPS = NODES // 16
LOCAL = 8
REMOTE = 8
VMEM = pl.BlockSpec(memory_space=pltpu.VMEM)
HBM = pl.BlockSpec(memory_space=pltpu.HBM)
DMA = pltpu.SemaphoreType.DMA
BLOCK = 256
BLOCKS = NODES // BLOCK
MESSAGE = 40
CUTS = (0, 256, 768, 1280, 2048)
STEPS = len(CUTS) - 1
PIECES = {3: (0, 4), 6: (4, 7), 7: (7, 8)}
FINISH_PIECE = 2
NN = (((1,), (0,)), ((), ()))
NT = (((1,), (1,)), ((), ()))
TN = (((0,), (0,)), ((), ()))


def dot(a, b, dims=NN):
    return lax.dot_general(a, b, dims, preferred_element_type=F32)


def one_hot(keys, shape, axis):
    return jnp.where(keys == lax.broadcasted_iota(I32, shape, axis), F32(1), F32(0)).astype(BF16)


def in_hbm(*arrays):
    return [pltpu.with_memory_space_constraint(array, pltpu.HBM) for array in arrays]


def start(source, target, semaphore, priority=0):
    copy = pltpu.make_async_copy(source, target, semaphore)
    copy.start(priority=priority)
    return copy


def rows_of(block):
    return pl.ds(block * BLOCK, BLOCK)


def flatten_lanes(values):
    k, n = values.shape
    per = 256 // k
    lane = lax.broadcasted_iota(I32, (k, 256), 1)
    own = lax.broadcasted_iota(I32, (k, 256), 0) == (lane & (k - 1))
    tiled = dot(values.astype(BF16), jnp.where(own, F32(1), F32(0)).astype(BF16), TN)
    shape = (n // per, per, 256)
    shift = k.bit_length() - 1
    mine = (lax.broadcasted_iota(I32, shape, 2) >> shift) == lax.broadcasted_iota(I32, shape, 1)
    return jnp.sum(jnp.where(mine, tiled.reshape(shape), F32(0)), axis=1)


def pack_kernel(features_hbm, lists_hbm, hub_hbm, packed, features, lists, hub, sems):
    get_lists = start(lists_hbm, lists, sems.at[0])
    get_hub = start(hub_hbm, hub, sems.at[1])
    get_features = start(features_hbm, features, sems.at[2])
    get_lists.wait()
    get_hub.wait()
    get_features.wait()
    ids = flatten_lanes((lists[...] >> 8).astype(F32)) * 256.0 + flatten_lanes(
        (lists[...] & 255).astype(F32)
    )
    hub_ids = jnp.concatenate([hub[...].astype(F32), jnp.full((1, 120), -1.0, F32)], axis=1)
    ids = jnp.concatenate([ids[part : part + 1] for part in range(4)] + [hub_ids], axis=1)
    rows = lax.broadcasted_iota(I32, (256, 1152), 0).astype(F32).astype(BF16)
    picked = jnp.zeros((1152, WIDTH), F32)
    for chunk in range(8):
        offset = ids - chunk * 256.0
        inside = (offset >= 0.0) & (offset < 256.0)
        keys = jnp.where(inside, offset, -1.0).astype(BF16)
        hot = jnp.where(jnp.broadcast_to(keys, (256, 1152)) == rows, BF16(1), BF16(0))
        picked = picked + dot(hot, features[chunk * 256 : (chunk + 1) * 256, :], TN)
    hubs = jnp.broadcast_to(picked[8 * PEERS : 8 * PEERS + 8][None], (PEERS, 8, WIDTH))
    bound = picked[: 8 * PEERS].reshape(PEERS, 8, WIDTH)
    packed[...] = jnp.concatenate([bound, hubs], axis=1).astype(BF16)


def pack(features, lists, hub):
    return pl.pallas_call(
        pack_kernel,
        out_shape=pltpu.HBM((PEERS, SLOTS, WIDTH), BF16),
        in_specs=[HBM] * 3,
        out_specs=VMEM,
        scratch_shapes=[
            pltpu.VMEM((NODES, WIDTH), BF16),
            pltpu.VMEM((8, PEERS), I32),
            pltpu.VMEM((1, 8), I32),
            DMA((3,)),
        ],
        compiler_params=pltpu.CompilerParams(vmem_limit_bytes=24 << 20),
        cost_estimate=pl.CostEstimate(
            flops=2 * 1040 * NODES * WIDTH, bytes_accessed=2 << 20, transcendentals=0
        ),
        name="pack",
    )(*in_hbm(features, lists, hub))


CHUNK = 512
CHUNKS = NODES // CHUNK


def count_kernel(
    neighbours_hbm,
    counts_hbm,
    features_hbm,
    table_hbm,
    summed_hbm,
    neighbours,
    counts,
    features,
    table,
    summed,
    key_hi,
    key_lo,
    in_sems,
    table_sems,
    summed_sems,
):
    get_neighbours = start(neighbours_hbm, neighbours, in_sems.at[0])
    get_counts = start(counts_hbm, counts, in_sems.at[1])
    get_features = start(features_hbm, features, in_sems.at[2])
    get_neighbours.wait()
    index = neighbours[...]
    bound = index - NODES
    hub = bound - 8 * PEERS
    index = jnp.where(
        index < NODES,
        index,
        jnp.where(
            hub < 0,
            NODES + ((bound >> 3) << 4) + (bound & 7),
            NODES + ((hub >> 3) << 4) + 8 + (hub & 7),
        ),
    )
    get_counts.wait()
    usable = lax.broadcasted_iota(I32, index.shape, 0) < counts[...]
    index = jnp.where(usable, index, 4096)
    lane = lax.broadcasted_iota(I32, (GROUPS, 256), 1)
    key_hi[...] = flatten_lanes((index >> 8).astype(F32)) * 16.0 + (lane >> 4).astype(F32)
    key_lo[...] = flatten_lanes((index & 255).astype(F32))
    get_features.wait()

    rows = lax.broadcasted_iota(I32, (256, 256), 0).astype(F32).astype(BF16)

    def products(group):
        hi = jnp.broadcast_to(key_hi[pl.ds(group, 1), :].astype(BF16), (256, 256))
        lo = jnp.broadcast_to(key_lo[pl.ds(group, 1), :].astype(BF16), (256, 256))
        left = jnp.where(hi == rows, BF16(1), BF16(0)).astype(PRODUCT)
        right = jnp.where(lo == rows, BF16(1), BF16(0)).astype(PRODUCT)
        return dot(left, right, NT).reshape(16, 16, 256)

    def one_pair(pair, carry):
        both = jnp.concatenate([products(2 * pair), products(2 * pair + 1)], axis=1)
        at = pl.ds(pl.multiple_of(pair * 32, 32), 32)
        table[:, at, :] = both.astype(COUNT)
        return carry

    copies = []
    for chunk in range(CHUNKS):
        lax.fori_loop(
            chunk * CHUNK // 32, (chunk + 1) * CHUNK // 32, one_pair, 0, unroll=UNROLL
        )
        at = pl.ds(chunk * CHUNK, CHUNK)
        copies.append(start(table.at[:, at], table_hbm.at[:, at], table_sems.at[chunk]))
    for half in range(2):
        for block in range(2 * half, 2 * half + 2):
            at = slice(block * 512, (block + 1) * 512)
            total = jnp.zeros((512, WIDTH), F32)
            for hi in range(LOCAL):
                total = total + dot(
                    table[hi, at, :].astype(BF16), features[hi * 256 : (hi + 1) * 256, :]
                )
            summed[at, :] = total
        at = pl.ds(half * 1024, 1024)
        copies.append(start(summed.at[at], summed_hbm.at[at], summed_sems.at[half]))
    for copy in copies:
        copy.wait()


def count(neighbours, counts, features):
    return pl.pallas_call(
        count_kernel,
        out_shape=(
            pltpu.HBM((LOCAL + REMOTE, NODES, WIDTH), COUNT),
            pltpu.HBM((NODES, WIDTH), F32),
        ),
        in_specs=[HBM] * 3,
        out_specs=[HBM] * 2,
        scratch_shapes=[
            pltpu.VMEM((FAN, NODES), I32),
            pltpu.VMEM((1, NODES), I32),
            pltpu.VMEM((NODES, WIDTH), BF16),
            pltpu.VMEM((LOCAL + REMOTE, NODES, WIDTH), COUNT),
            pltpu.VMEM((NODES, WIDTH), F32),
            pltpu.VMEM((GROUPS, 256), F32),
            pltpu.VMEM((GROUPS, 256), F32),
            DMA((3,)),
            DMA((CHUNKS,)),
            DMA((CHUNKS,)),
        ],
        compiler_params=pltpu.CompilerParams(vmem_limit_bytes=40 << 20),
        cost_estimate=pl.CostEstimate(
            flops=2 * NODES * 4096 * WIDTH * 2, bytes_accessed=20 << 20, transcendentals=0
        ),
        name="count",
    )(*in_hbm(neighbours, counts, features))


def node_kernel(
    arrived,
    table_hbm,
    summed_hbm,
    features_hbm,
    counts_hbm,
    cotangent_hbm,
    self_weight_hbm,
    neighbour_weight_hbm,
    activations_hbm,
    grad_pre_hbm,
    edge_hbm,
    message_hbm,
    table,
    summed,
    features,
    counts,
    cotangent,
    self_weight,
    neighbour_weight,
    activations,
    grad_pre,
    edge,
    mean,
    message,
    weights,
    parts,
    small_sems,
    in_sems,
    out_sems,
    message_sems,
):
    get_small = [
        start(counts_hbm, counts, small_sems.at[0]),
        start(self_weight_hbm, self_weight, small_sems.at[1]),
        start(neighbour_weight_hbm, neighbour_weight, small_sems.at[2]),
    ]
    get = []
    for step in range(STEPS):
        at = pl.ds(CUTS[step], CUTS[step + 1] - CUTS[step])
        late = min(step, 1)
        get.append(
            [
                start(
                    table_hbm.at[pl.ds(LOCAL, REMOTE), at],
                    table.at[:, at],
                    in_sems.at[1, step],
                    late,
                ),
                start(summed_hbm.at[at], summed.at[at], in_sems.at[2, step], late),
                start(features_hbm.at[at], features.at[at], in_sems.at[0, step], late),
                start(cotangent_hbm.at[at], cotangent.at[at], in_sems.at[3, step], late),
            ]
        )
    for copy in get_small:
        copy.wait()
    inverse = (1.0 / counts[...].astype(F32)).T
    remote = arrived[...].reshape(NODES, WIDTH)
    scales = [
        jnp.concatenate(
            [
                jnp.broadcast_to(inverse[:, part : part + 1], (128, 256))
                for part in range(CUTS[step] // 128, CUTS[step + 1] // 128)
            ],
            axis=0,
        )
        for step in range(STEPS)
    ]

    def gather(step):
        for copy in get[step]:
            copy.wait()
        at = slice(CUTS[step], CUTS[step + 1])
        total = summed[at, :]
        for hi in range(REMOTE):
            total = total + dot(table[hi, at, :].astype(BF16), remote[hi * 256 : (hi + 1) * 256])
        return (total * scales[step]).astype(BF16)

    def update(step, block_mean):
        at = slice(CUTS[step], CUTS[step + 1])
        mean[at, :] = block_mean
        pre = dot(features[at, :], self_weight[...]) + dot(block_mean, neighbour_weight[...])
        sigmoid = 0.5 * jnp.tanh(0.5 * pre) + 0.5
        activations[at, :] = (pre * sigmoid).astype(BF16)
        slope = sigmoid * (1.0 + pre * (1.0 - sigmoid))
        block_grad = (cotangent[at, :].astype(F32) * slope).astype(BF16)
        grad_pre[at, :] = block_grad
        edge[at, :] = (dot(block_grad, neighbour_weight[...], NT) * scales[step]).astype(BF16)
        for part, left in ((0, features[at, :]), (1, block_mean)):
            product = dot(left, block_grad, TN)
            for half in range(2):
                where = (half, slice(part * WIDTH, (part + 1) * WIDTH))
                piece = product[:, half * 128 : (half + 1) * 128]
                weights[where] = piece if step == 0 else weights[where] + piece

    now = gather(0)
    for step in range(STEPS):
        later = gather(step + 1) if step + 1 < STEPS else None
        update(step, now)
        now = later
    put = []
    for half in range(2):
        for row in range(4):
            parts[pl.ds(half * 4 + row, PEERS, stride=8), :] = weights[
                half, pl.ds(row, PEERS, stride=4), :
            ]
    message[:, 32:40, :] = parts[: 8 * PEERS, :].reshape(PEERS, 8, 128).astype(BF16)
    put = [
        start(activations, activations_hbm, out_sems.at[0], 1),
        start(grad_pre, grad_pre_hbm, out_sems.at[1], 1),
        start(edge, edge_hbm, out_sems.at[2], 1),
    ]
    for hi in range(REMOTE):
        added = dot(table[hi].astype(BF16), edge[...], TN).astype(BF16).reshape(16, 16, WIDTH)
        message[hi * 16 : (hi + 1) * 16, 0:16, :] = added[:, :, :128]
        message[hi * 16 : (hi + 1) * 16, 16:32, :] = added[:, :, 128:]
        if hi in PIECES:
            first, last = PIECES[hi]
            peers = pl.ds(first * 16, (last - first) * 16)
            put.append(start(message.at[peers], message_hbm.at[peers], message_sems.at[hi]))
    for copy in put:
        copy.wait()


def node(
    arrived, table, summed, features, counts, cotangent, self_weight, neighbour_weight
):
    rows = pltpu.VMEM((NODES, WIDTH), BF16)
    return pl.pallas_call(
        node_kernel,
        out_shape=(
            pltpu.HBM((NODES, WIDTH), BF16),
            pltpu.HBM((NODES, WIDTH), BF16),
            pltpu.HBM((NODES, WIDTH), BF16),
            pltpu.HBM((PEERS, MESSAGE, 128), BF16),
        ),
        in_specs=[VMEM] + [HBM] * 7,
        out_specs=[HBM] * 4,
        scratch_shapes=[
            pltpu.VMEM((REMOTE, NODES, WIDTH), COUNT),
            pltpu.VMEM((NODES, WIDTH), F32),
            rows,
            pltpu.VMEM((16, 128), I32),
            rows,
            pltpu.VMEM((WIDTH, WIDTH), BF16),
            pltpu.VMEM((WIDTH, WIDTH), BF16),
            rows,
            rows,
            rows,
            rows,
            pltpu.VMEM((PEERS, MESSAGE, 128), BF16),
            pltpu.VMEM((2, 2 * WIDTH + 8, 128), F32),
            pltpu.VMEM((8 * PEERS + 8, 128), F32),
            DMA((3,)),
            DMA((4, STEPS)),
            DMA((3,)),
            DMA((REMOTE,)),
        ],
        compiler_params=pltpu.CompilerParams(vmem_limit_bytes=40 << 20),
        cost_estimate=pl.CostEstimate(
            flops=2 * NODES * 2048 * WIDTH * 2, bytes_accessed=16 << 20, transcendentals=0
        ),
        name="node",
    )(
        arrived,
        *in_hbm(table, summed, features, counts, cotangent, self_weight, neighbour_weight),
    )


def local_kernel(
    table_hbm,
    edge_hbm,
    grad_pre_hbm,
    self_weight_hbm,
    lists_hbm,
    grads_hbm,
    ids,
    table,
    edge,
    grad_pre,
    self_weight,
    lists,
    grads,
    in_sems,
    table_sems,
    out_sems,
):
    get_edge = start(edge_hbm, edge, in_sems.at[0])
    get = [start(table_hbm.at[hi], table.at[hi], table_sems.at[hi]) for hi in range(LOCAL)]
    get_small = [
        start(grad_pre_hbm, grad_pre, in_sems.at[1]),
        start(self_weight_hbm, self_weight, in_sems.at[2]),
        start(lists_hbm, lists, in_sems.at[3]),
    ]
    for copy in get_small:
        copy.wait()
    ids[...] = flatten_lanes((lists[...] >> 8).astype(F32)) * 256.0 + flatten_lanes(
        (lists[...] & 255).astype(F32)
    )
    get_edge.wait()
    for copy in get:
        copy.wait()
    for hi in range(LOCAL):
        at = slice(hi * 256, (hi + 1) * 256)
        grads[at, :] = dot(table[hi].astype(BF16), edge[...], TN) + dot(grad_pre[at, :], self_weight[...], NT)
    start(grads, grads_hbm, out_sems.at[0]).wait()


def local(table, edge, grad_pre, self_weight, lists):
    rows = pltpu.VMEM((NODES, WIDTH), BF16)
    return pl.pallas_call(
        local_kernel,
        out_shape=(
            pltpu.HBM((NODES, WIDTH), F32),
            pltpu.HBM((4, 256), F32),
        ),
        in_specs=[HBM] * 5,
        out_specs=[HBM, VMEM],
        scratch_shapes=[
            pltpu.VMEM((LOCAL, NODES, WIDTH), COUNT),
            rows,
            rows,
            pltpu.VMEM((WIDTH, WIDTH), BF16),
            pltpu.VMEM((8, PEERS), I32),
            pltpu.VMEM((NODES, WIDTH), F32),
            DMA((4,)),
            DMA((LOCAL,)),
            DMA((1,)),
        ],
        compiler_params=pltpu.CompilerParams(vmem_limit_bytes=40 << 20),
        cost_estimate=pl.CostEstimate(
            flops=2 * NODES * 2048 * WIDTH, bytes_accessed=14 << 20, transcendentals=0
        ),
        name="local",
    )(*in_hbm(table, edge, grad_pre, self_weight, lists))


def finish_kernel(
    returned,
    grads_hbm,
    ids_hbm,
    hub_hbm,
    grad_features_hbm,
    grad_weights,
    grads,
    ids,
    hub,
    totals,
    sems,
    put_sems,
):
    get_ids = start(ids_hbm, ids, sems.at[0])
    get_hub = start(hub_hbm, hub, sems.at[1])
    get_grads = start(grads_hbm, grads, sems.at[2])
    sides = [returned[:, 0:16, :].astype(F32), returned[:, 16:32, :].astype(F32)]
    bound = jnp.concatenate([side[:, :8].reshape(8 * PEERS, 128) for side in sides], axis=1)
    bound = bound.astype(BF16)
    hubs = jnp.concatenate([jnp.sum(side[:, 8:], axis=0) for side in sides], axis=1)
    high = hubs.astype(BF16).astype(F32)
    hubs = jnp.concatenate([high, hubs - high], axis=0).astype(BF16)
    weights = jnp.sum(returned[:, 32:40, :].astype(F32), axis=0)
    grad_weights[...] = jnp.concatenate([weights[:4], weights[4:]], axis=1)
    get_ids.wait()
    get_hub.wait()
    put = []
    rows = lax.broadcasted_iota(I32, (BLOCK, 256), 0).astype(F32).astype(BF16)
    twice = jnp.concatenate([hub[...], hub[...]], axis=1)
    for block in range(BLOCKS):
        at = slice(block * BLOCK, (block + 1) * BLOCK)
        offset = ids[...] - block * 256.0
        inside = (offset >= 0.0) & (offset < 256.0)
        keys = jnp.where(inside, offset, -1.0).astype(BF16)
        hot = jnp.concatenate(
            [
                jnp.where(
                    jnp.broadcast_to(keys[part : part + 1, :], (BLOCK, 256)) == rows,
                    BF16(1),
                    BF16(0),
                )
                for part in range(4)
            ],
            axis=1,
        )
        hub_hot = one_hot(
            jnp.broadcast_to(twice - block * BLOCK, (BLOCK, 16)), (BLOCK, 16), 0
        )
        added = dot(hot, bound) + dot(hub_hot, hubs)
        if block == 0:
            get_grads.wait()
        totals[at, :] = grads[at, :] + added
        if (block + 1) % FINISH_PIECE == 0:
            piece = pl.ds((block + 1 - FINISH_PIECE) * BLOCK, FINISH_PIECE * BLOCK)
            put.append(start(totals.at[piece], grad_features_hbm.at[piece], put_sems.at[block]))
    for copy in put:
        copy.wait()


def finish(returned, grads, ids, hub):
    return pl.pallas_call(
        finish_kernel,
        out_shape=(
            pltpu.HBM((NODES, WIDTH), F32),
            jax.ShapeDtypeStruct((4, WIDTH), F32),
        ),
        in_specs=[VMEM, HBM, HBM, HBM],
        out_specs=[HBM, VMEM],
        scratch_shapes=[
            pltpu.VMEM((NODES, WIDTH), F32),
            pltpu.VMEM((4, 256), F32),
            pltpu.VMEM((1, 8), I32),
            pltpu.VMEM((NODES, WIDTH), F32),
            DMA((3,)),
            DMA((BLOCKS,)),
        ],
        compiler_params=pltpu.CompilerParams(vmem_limit_bytes=32 << 20),
        cost_estimate=pl.CostEstimate(
            flops=2 * NODES * 1024 * WIDTH, bytes_accessed=6 << 20, transcendentals=0
        ),
        name="finish",
    )(returned, *in_hbm(grads, ids, hub))


def body(
    features, self_weight, neighbour_weight, send_lists, hub_nodes, neighbours, counts, cotangent
):
    lists = send_lists[0].T
    packed = pack(features, lists, hub_nodes)
    arrived = lax.all_to_all(packed, "dom", split_axis=0, concat_axis=0, tiled=True)
    table, summed = count(neighbours.T, counts.reshape(1, NODES), features)
    activations, grad_pre, edge, message = node(
        arrived,
        table,
        summed,
        features,
        counts.reshape(16, 128),
        cotangent,
        self_weight,
        neighbour_weight,
    )
    returned = lax.all_to_all(message, "dom", split_axis=0, concat_axis=0, tiled=True)
    grads, ids = local(table, edge, grad_pre, self_weight, lists)
    grad_features, grad_weights = finish(returned, grads, ids, hub_nodes)
    return (activations, grad_features, grad_weights)


def solution(mesh):
    in_specs = (
        P("dom", None),
        P(),
        P(),
        P("dom", None, None),
        P("dom", None),
        P("dom", None),
        P("dom"),
        P("dom", None),
    )
    out_specs = (P("dom", None), P("dom", None), P("dom", None))
    return jax.shard_map(body, mesh=mesh, in_specs=in_specs, out_specs=out_specs, check_vma=False)
```
